128 devices in a mesh: ctx: 32 (over z, y, x_hi), tp: 4 (over x_lo, core).
Axes of the slice: x: 4 (x_hi: 2, x_lo: 2; x = x_hi * 2 + x_lo), y: 4, z: 4, core: 2. Of those that a mesh axis runs over, the one named last changes fastest.
Arguments:
- branches: bfloat16 [3, 4096, 4096], P(None, 'ctx', 'tp'), may hold values from -6 to 6
- short_taps: float32 [3, 3, 4096], replicated, may hold values from -2.5 to 2.5
- long_filter: float32 [4096, 4096], P(('tp', 'ctx')), may hold values from 0 to 26.487934, as said below
- grad_out: bfloat16 [4096, 4096], P('ctx', 'tp'), may hold values from -6 to 6
Outputs:
- grad_branches: bfloat16 [3, 4096, 4096], P(None, 'ctx', 'tp')
- grad_filter: float32 [4096, 4096], P(('tp', 'ctx'))
The draws below stay inside these ranges and needn't reach their ends.
Inputs may be any that keep to these rules, and one draw needn't show every extreme that they name: `long_filter`: positive filter values, applied after division by the square root of 4096.
All inputs are finite; a program needn't handle non-finite values.
Results may differ from the reference program's by a relative error of at most 0.014.
Values may be sent and summed in bfloat16 or wider, within the bound.
No kernel may reach another device: no remote copies, remote signals or barrier semaphores. Data moves between devices by JAX's collectives and lax.ppermute only.
A program may use at most 64 MiB of HBM per device.

```python
import math
import jax
import jax.numpy as jnp
from jax import lax

MIXER_FEATURES = 4096
SHORT = 3
SEQUENCE_EXTENT = 4096


def draw_long_filter(key, part):
    key = jax.random.fold_in(key, 7)
    subkeys = jax.random.split(key, 5)
    log_rate = jax.random.uniform(subkeys[1], (MIXER_FEATURES, 1), minval=math.log(1.0 / (2.0 * SEQUENCE_EXTENT)), maxval=math.log(1.0 / 30.0))
    lowest, highest = (0.5, 1.5)
    kernel_falloff = jnp.exp(log_rate)
    delay_sizes = jnp.arange(SEQUENCE_EXTENT, dtype=jnp.float32)[None, :]
    kernel_magnitude = jnp.sqrt(2.0 * kernel_falloff / (1.0 - jnp.exp(-2.0 * kernel_falloff * SEQUENCE_EXTENT))) * math.sqrt(SEQUENCE_EXTENT)
    sequence_places = jax.random.randint(subkeys[2], (MIXER_FEATURES, 3), 1, SEQUENCE_EXTENT)
    omitted_items = jax.random.uniform(subkeys[3], (MIXER_FEATURES, 3), minval=0.5, maxval=0.8)
    delay_place = jnp.arange(SEQUENCE_EXTENT, dtype=jnp.int32)[None, :]
    impulse_cluster = jnp.ones((MIXER_FEATURES, SEQUENCE_EXTENT), jnp.float32)
    for vertical_band in range(3):
        impulse_cluster = impulse_cluster * jnp.where(delay_place >= sequence_places[:, vertical_band:vertical_band + 1], omitted_items[:, vertical_band:vertical_band + 1], 1.0)
    rough_guess = jax.random.uniform(subkeys[4], (MIXER_FEATURES, SEQUENCE_EXTENT), minval=lowest, maxval=highest)
    return (kernel_magnitude * jnp.exp(-kernel_falloff * delay_sizes) * impulse_cluster * rough_guess).astype(jnp.float32)


def block_levels(rng, shape, pieces, least, largest):
    loudness = 1.0
    for dim, parts in pieces:
        steps = jax.random.uniform(jax.random.fold_in(jax.random.fold_in(rng, 6), dim), (parts,), jnp.float32, least / len(pieces), largest / len(pieces))
        loudness = loudness * jnp.repeat(jnp.exp(steps), shape[dim] // parts).reshape((-1,) + (1,) * (len(shape) - 1 - dim))
    return loudness


def scatter_about(rng, dims, width, limit, pieces=(), held_as=jnp.bfloat16):
    array = jax.random.normal(rng, dims, jnp.float32) * width
    if len(pieces) > 0:
        array = block_levels(rng, dims, pieces, -0.22, 0.18) * array
    return jnp.clip(array, min=-limit, max=limit).astype(held_as)


def setup_inputs(seed: int = 0) -> dict:
    seeds = jax.random.split(jax.random.key(seed), 5)
    branches = scatter_about(seeds[0], (3, SEQUENCE_EXTENT, MIXER_FEATURES), 1.0, 6.0, ((1, 32), (2, 4)))
    short_taps = scatter_about(seeds[1], (3, SHORT, MIXER_FEATURES), 0.6, 2.5, (), jnp.float32)
    long_filter = draw_long_filter(jax.random.fold_in(seeds[4], 71), 0)
    grad_out = scatter_about(seeds[3], (SEQUENCE_EXTENT, MIXER_FEATURES), 1.0, 6.0, ((0, 32), (1, 4)))
    return dict(branches=branches, short_taps=short_taps, long_filter=long_filter, grad_out=grad_out)


def featurize(branches, short_taps):
    length = branches.shape[1]
    span = short_taps.shape[1]
    padded = jnp.pad(branches.astype(jnp.float32), ((0, 0), (span - 1, 0), (0, 0)))
    total = jnp.zeros(branches.shape, jnp.float32)
    for offset in range(span):
        start = span - 1 - offset
        total = total + short_taps[:, offset, None, :] * padded[:, start:start + length, :]
    return total.astype(jnp.bfloat16)


def adjoint_taps(grads, short_taps):
    length = grads.shape[1]
    span = short_taps.shape[1]
    padded = jnp.pad(grads.astype(jnp.float32), ((0, 0), (0, span - 1), (0, 0)))
    total = jnp.zeros(grads.shape, jnp.float32)
    for offset in range(span):
        total = total + short_taps[:, offset, None, :] * padded[:, offset:offset + length, :]
    return total.astype(jnp.bfloat16)


def block_conv(operands):
    zeta_block, gate_block, filter_block = operands
    length = zeta_block.shape[-1]
    size = 2 * length
    zeta_freq = jnp.fft.rfft(zeta_block, n=size, axis=-1)
    gate_freq = jnp.fft.rfft(gate_block, n=size, axis=-1)
    filter_freq = jnp.fft.rfft(filter_block, n=size, axis=-1)
    conv = jnp.fft.irfft(filter_freq * zeta_freq, n=size, axis=-1)[:, :length]
    dzeta = jnp.fft.irfft(jnp.conj(filter_freq) * gate_freq, n=size, axis=-1)[:, :length]
    dfilter = jnp.fft.irfft(jnp.conj(zeta_freq) * gate_freq, n=size, axis=-1)[:, :length]
    return conv, dzeta, dfilter


def multiply(left, right):
    return (left.astype(jnp.float32) * right.astype(jnp.float32)).astype(jnp.bfloat16)


def reference(branches, short_taps, long_filter, grad_out):
    feats = featurize(branches, short_taps)
    query_rows, key_rows, value_rows = feats[0], feats[1], feats[2]
    products = multiply(key_rows, value_rows)
    gate_grad = multiply(grad_out, query_rows)
    scale = SEQUENCE_EXTENT ** -0.5
    blocks = MIXER_FEATURES // 128

    def to_blocks(matrix):
        return matrix.astype(jnp.float32).T.reshape(blocks, 128, SEQUENCE_EXTENT)

    filter_blocks = (long_filter * scale).reshape(blocks, 128, SEQUENCE_EXTENT)
    conv, dzeta, dfilter = lax.map(block_conv, (to_blocks(products), to_blocks(gate_grad), filter_blocks))
    conv = conv.reshape(MIXER_FEATURES, SEQUENCE_EXTENT).T.astype(jnp.bfloat16)
    dzeta = dzeta.reshape(MIXER_FEATURES, SEQUENCE_EXTENT).T.astype(jnp.bfloat16)
    grad_filter = dfilter.reshape(MIXER_FEATURES, SEQUENCE_EXTENT) * scale
    dfeat = jnp.stack([multiply(grad_out, conv), multiply(dzeta, value_rows), multiply(dzeta, key_rows)])
    grad_branches = adjoint_taps(dfeat, short_taps)
    return grad_branches, grad_filter
```

```python
import functools

import jax
import jax.numpy as jnp
import ml_dtypes
import numpy as np
from jax import lax
from jax.experimental import pallas as pl
from jax.experimental.pallas import tpu as pltpu
from jax.sharding import PartitionSpec as P

F32 = jnp.float32
BF16 = jnp.bfloat16
CHUNK = 128
BLOCKS = 32
GROUP = 16
HALF = BLOCKS
PERIOD = 2 * BLOCKS * CHUNK
ROWS = 80
CB = 256


@functools.lru_cache(maxsize=None)
def tables():
    bf = ml_dtypes.bfloat16
    k = np.arange(HALF)[:, None] + 0.5
    m = np.arange(BLOCKS)[None, :]
    eye = np.eye(GROUP)
    phase = 2 * np.pi * k * m / (2 * BLOCKS)
    first = np.stack([np.cos(phase), -np.sin(phase)])
    lhs1 = np.einsum("qkm,st->qskmt", first, eye).reshape(2 * GROUP * HALF, BLOCKS * GROUP)
    last = np.stack([np.cos(phase), -np.sin(phase)]) * (2.0 / PERIOD)
    lhs2 = np.einsum("qkm,st->msqtk", last, eye).reshape(BLOCKS * GROUP, 2 * GROUP * HALF)
    r = np.arange(CHUNK)
    cr = 2 * np.pi * (np.outer(r, r) % CHUNK) / CHUNK
    c, s = np.cos(cr), np.sin(cr)
    fwd = np.block([[c, -s], [s, c]])
    inv = np.block([[c, s], [-s, c]])
    tw = 2 * np.pi * k * r[None, :] / PERIOD
    twist = np.stack([np.cos(tw), -np.sin(tw)]).astype(np.float32)
    return lhs1.astype(bf), lhs2.astype(bf), fwd.astype(bf), inv.astype(bf), twist


def dot(a, b):
    return jnp.dot(a, b, preferred_element_type=F32)


def head_kernel(taps_ref, br_ref, go_ref, send_ref, key_ref, val_ref):
    base = (lax.axis_index("tp") * pl.num_programs(0) + pl.program_id(0)) * CB
    cols = pl.ds(pl.multiple_of(base, CB), CB)
    row = lax.broadcasted_iota(jnp.int32, (CHUNK, CB), 0)
    row8 = lax.broadcasted_iota(jnp.int32, (8, CB), 0)
    feats, tails = [], []
    for b in range(3):
        x = br_ref[b].astype(F32)
        s0, s1, s2 = (taps_ref[b, j : j + 1, cols] for j in range(3))
        x1 = pltpu.roll(x, 1, 0)
        x2 = pltpu.roll(x, 2, 0)
        feats.append(s0 * x + s1 * jnp.where(row < 1, 0.0, x1) + s2 * jnp.where(row < 2, 0.0, x2))
        tails.append(
            jnp.where(row8 < 1, s1 * x1[:8], 0.0) + jnp.where(row8 < 2, s2 * x2[:8], 0.0)
        )
    query, key, value = feats
    go = go_ref[...].astype(F32)
    key_ref[...] = key.astype(BF16)
    val_ref[...] = value.astype(BF16)
    nd = CB // 32
    send_ref[:, 0:32, :] = (key * value).T.astype(BF16).reshape(nd, 32, CHUNK)
    send_ref[:, 32:64, :] = (go * query).T.astype(BF16).reshape(nd, 32, CHUNK)
    heads = jnp.where(
        row8 < 2,
        query[:8],
        jnp.where(
            row8 < 4,
            pltpu.roll(key[:8], 2, 0),
            jnp.where(row8 < 6, pltpu.roll(value[:8], 4, 0), pltpu.roll(go[:8], 6, 0)),
        ),
    )
    ends = jnp.where(
        row8 < 2,
        tails[0],
        jnp.where(row8 < 4, pltpu.roll(tails[1], 2, 0), pltpu.roll(tails[2], 4, 0)),
    )
    upper = lax.broadcasted_iota(jnp.int32, (8, CB), 1) // GROUP % 2 == 1
    padded = jnp.concatenate(
        [
            jnp.where(upper, 0.0, heads),
            jnp.where(upper, 0.0, ends),
            jnp.where(upper, heads, 0.0),
            jnp.where(upper, ends, 0.0),
            jnp.zeros((CHUNK - 32, CB), F32),
        ],
        axis=0,
    )
    turned = padded.T.reshape(nd, 2, GROUP, CHUNK)
    send_ref[:, 64:80, :] = (turned[:, 0] + turned[:, 1]).astype(BF16)


def twisted(real, imag, twist_ref, sign):
    shape = real.shape
    real = real.reshape(GROUP, HALF, CHUNK)
    imag = imag.reshape(GROUP, HALF, CHUNK)
    c = twist_ref[0]
    s = twist_ref[1] * sign
    out_r = (real * c - imag * s).astype(BF16).reshape(shape)
    out_i = (real * s + imag * c).astype(BF16).reshape(shape)
    return out_r, out_i


def forward(first, twist_ref, fwd_ref):
    half = GROUP * HALF
    re, im = twisted(first[:half], first[half:], twist_ref, 1.0)
    return dot(jnp.concatenate([re, im], axis=1), fwd_ref[...])


def backward(spectrum, twist_ref, inv_ref):
    value = dot(spectrum, inv_ref[...])
    re, im = twisted(value[:, :CHUNK], value[:, CHUNK:], twist_ref, -1.0)
    return jnp.concatenate([re, im], axis=0)


def filter_kernel(filter_ref, lhs1_ref, fwd_ref, twist_ref, out_ref):
    scale = (BLOCKS * CHUNK) ** -0.5
    for j in range(2):
        rows = filter_ref[GROUP * j : GROUP * (j + 1), :]
        stacked = jnp.concatenate(
            [rows[:, CHUNK * m : CHUNK * (m + 1)] for m in range(BLOCKS)], axis=0
        )
        first = dot(lhs1_ref[...], (stacked * scale).astype(BF16))
        out_ref[j] = forward(first, twist_ref, fwd_ref).astype(BF16)


def middle_kernel(
    recv_ref, spec_ref, lhs1_ref, lhs2_ref, fwd_ref, inv_ref, twist_ref, send_ref, corr_ref
):
    shape = (BLOCKS, GROUP, CHUNK)
    flat = (BLOCKS * GROUP, CHUNK)
    lane = lax.broadcasted_iota(jnp.int32, (GROUP, CHUNK), 1)
    turn = lambda x, by: pltpu.roll(x, by % CHUNK, 2)
    halo = recv_ref[:, 64:80, :].astype(F32)
    before = jnp.concatenate([jnp.zeros((1, GROUP, CHUNK), F32), halo[:-1]], axis=0)
    feat = halo + turn(before, -8)
    prod = turn(feat, -2) * turn(feat, -4)
    gate = feat * turn(halo, -6)
    spectra = []
    for at, fix in ((0, prod), (32, gate)):
        pair = []
        for j in range(2):
            x = recv_ref[:, at + GROUP * j : at + GROUP * (j + 1), :].astype(F32)
            head = fix if j == 0 else turn(fix, -GROUP)
            pair.append(jnp.where(lane < 2, head, x).astype(BF16).reshape(flat))
        first = dot(lhs1_ref[...], jnp.concatenate(pair, axis=1))
        spectra.append(
            [forward(first[:, CHUNK * j : CHUNK * (j + 1)], twist_ref, fwd_ref) for j in range(2)]
        )
    outs = []
    for j in range(2):
        pr, pi = spectra[0][j][:, :CHUNK], spectra[0][j][:, CHUNK:]
        gr, gi = spectra[1][j][:, :CHUNK], spectra[1][j][:, CHUNK:]
        hr = spec_ref[j, :, :CHUNK].astype(F32)
        hi = spec_ref[j, :, CHUNK:].astype(F32)
        join = lambda re, im: jnp.concatenate([re.astype(BF16), im.astype(BF16)], axis=1)
        corr_ref[j] = join(pr * gr + pi * gi, pr * gi - pi * gr)
        conv = backward(join(hr * pr - hi * pi, hr * pi + hi * pr), twist_ref, inv_ref)
        dzeta = backward(join(hr * gr + hi * gi, hr * gi - hi * gr), twist_ref, inv_ref)
        both = dot(lhs2_ref[...], jnp.concatenate([conv, dzeta], axis=1))
        conv = both[:, :CHUNK].reshape(shape)
        dzeta = both[:, CHUNK:].reshape(shape)
        send_ref[:, GROUP * j : GROUP * (j + 1), :] = conv.astype(BF16)
        send_ref[:, 32 + GROUP * j : 32 + GROUP * (j + 1), :] = dzeta.astype(BF16)
        outs.append((conv, dzeta))
    conv = jnp.where(lane < GROUP, outs[0][0], turn(outs[1][0], GROUP))
    dzeta = jnp.where(lane < GROUP, outs[0][1], turn(outs[1][1], GROUP))
    place = lane % GROUP
    heads = jnp.where(
        place < 2,
        conv * turn(halo, -6),
        jnp.where(place < 4, turn(dzeta, 2) * turn(feat, -2), turn(dzeta, 4) * turn(feat, 2)),
    )
    after = jnp.concatenate([heads[1:], jnp.zeros((1, GROUP, CHUNK), F32)], axis=0)
    send_ref[:, 64:80, :] = jnp.where(place < 8, feat, turn(after, 8)).astype(BF16)


def grad_filter_kernel(corr_ref, lhs2_ref, inv_ref, twist_ref, out_ref):
    scale = (BLOCKS * CHUNK) ** -0.5
    stacked = jnp.concatenate(
        [backward(corr_ref[j], twist_ref, inv_ref) for j in range(2)], axis=1
    )
    both = dot(lhs2_ref[...], stacked) * scale
    for j in range(2):
        for m in range(BLOCKS):
            out_ref[GROUP * j : GROUP * (j + 1), CHUNK * m : CHUNK * (m + 1)] = both[
                GROUP * m : GROUP * (m + 1), CHUNK * j : CHUNK * (j + 1)
            ]


def tail_kernel(taps_ref, recv_ref, key_ref, val_ref, go_ref, out_ref):
    base = (lax.axis_index("tp") * pl.num_programs(0) + pl.program_id(0)) * CB
    cols = pl.ds(pl.multiple_of(base, CB), CB)
    row8 = lax.broadcasted_iota(jnp.int32, (8, CB), 0)
    conv = recv_ref[:, 0:32, :].astype(F32).reshape(CB, CHUNK).T
    dzeta = recv_ref[:, 32:64, :].astype(F32).reshape(CB, CHUNK).T
    halo = recv_ref[:, 64:80, :].astype(F32)
    halo = jnp.concatenate([halo, pltpu.roll(halo, CHUNK - GROUP, 2)], axis=1)
    halo = halo.reshape(CB, CHUNK).T
    heads, nexts = halo[:8], halo[8:16]

    def with_head(ref, at):
        value = ref[...].astype(F32)
        first = jnp.where(row8 < 2, pltpu.roll(heads, 8 - at, 0), value[:8])
        return jnp.concatenate([first, value[8:]], axis=0)

    key = with_head(key_ref, 2)
    value = with_head(val_ref, 4)
    grads = (go_ref[...].astype(F32) * conv, dzeta * value, dzeta * key)
    for b in range(3):
        d = grads[b]
        s0, s1, s2 = (taps_ref[b, j : j + 1, cols] for j in range(3))
        d1 = pltpu.roll(d, CHUNK - 1, 0)
        d2 = pltpu.roll(d, CHUNK - 2, 0)
        e1 = jnp.where(row8 < 7, d1[-8:], pltpu.roll(nexts, (7 - 2 * b) % 8, 0))
        e2 = jnp.where(row8 < 6, d2[-8:], pltpu.roll(nexts, (6 - 2 * b) % 8, 0))
        d1 = jnp.concatenate([d1[:-8], e1], axis=0)
        d2 = jnp.concatenate([d2[:-8], e2], axis=0)
        out_ref[b] = (s0 * d + s1 * d1 + s2 * d2).astype(BF16)


def params(mib):
    return pltpu.CompilerParams(vmem_limit_bytes=mib << 20)


def exchange(x):
    return lax.all_to_all(x, "ctx", split_axis=0, concat_axis=0, tiled=True)


def per_device(branches, short_taps, long_filter, grad_out):
    sds = jax.ShapeDtypeStruct
    lhs1, lhs2, fwd, inv, twist = (jnp.asarray(t) for t in tables())
    tokens, channels = grad_out.shape
    steps = channels // CB
    nd = CB // 32
    taps_spec = pl.BlockSpec(short_taps.shape, lambda i: (0, 0, 0))
    rows_spec = pl.BlockSpec((tokens, CB), lambda i: (0, i))
    branch_spec = pl.BlockSpec((3, tokens, CB), lambda i: (0, 0, i))
    wire_spec = pl.BlockSpec((nd, ROWS, CHUNK), lambda i: (i, 0, 0))
    wire = sds((BLOCKS, ROWS, CHUNK), BF16)
    half = GROUP * HALF
    send, key, value = pl.pallas_call(
        head_kernel,
        grid=(steps,),
        in_specs=[taps_spec, branch_spec, rows_spec],
        out_specs=[wire_spec, rows_spec, rows_spec],
        out_shape=[wire, sds((tokens, channels), BF16), sds((tokens, channels), BF16)],
        compiler_params=params(16),
        name="head",
    )(short_taps, branches, grad_out)
    spectrum = pl.pallas_call(
        filter_kernel,
        out_shape=sds((2, half, 2 * CHUNK), BF16),
        compiler_params=params(32),
        name="filter_spectrum",
    )(long_filter, lhs1, fwd, twist)
    recv = exchange(send)
    back, corr = pl.pallas_call(
        middle_kernel,
        out_shape=[wire, sds((2, half, 2 * CHUNK), BF16)],
        compiler_params=params(32),
        name="middle",
    )(recv, spectrum, lhs1, lhs2, fwd, inv, twist)
    grad_filter = pl.pallas_call(
        grad_filter_kernel,
        out_shape=sds(long_filter.shape, F32),
        compiler_params=params(32),
        name="grad_filter",
    )(corr, lhs2, inv, twist)
    returned = exchange(back)
    grads = pl.pallas_call(
        tail_kernel,
        grid=(steps,),
        in_specs=[taps_spec, wire_spec, rows_spec, rows_spec, rows_spec],
        out_specs=branch_spec,
        out_shape=sds(branches.shape, BF16),
        compiler_params=params(16),
        name="tail",
    )(short_taps, returned, key, value, grad_out)
    return grads, grad_filter


def solution(mesh):
    in_specs = (P(None, "ctx", "tp"), P(), P(("tp", "ctx"), None), P("ctx", "tp"))
    out_specs = (P(None, "ctx", "tp"), P(("tp", "ctx"), None))
    return jax.shard_map(
        per_device, mesh=mesh, in_specs=in_specs, out_specs=out_specs, check_vma=False
    )
```

```python
import functools

import jax
import jax.numpy as jnp
import ml_dtypes
import numpy as np
from jax import lax
from jax.experimental import pallas as pl
from jax.experimental.pallas import tpu as pltpu
from jax.sharding import PartitionSpec as P

F32 = jnp.float32
BF16 = jnp.bfloat16
CHUNK = 128
BLOCKS = 32
GROUP = 16
HALF = BLOCKS
PERIOD = 2 * BLOCKS * CHUNK
ROWS = 80
CB = 256


@functools.lru_cache(maxsize=None)
def tables():
    bf = ml_dtypes.bfloat16
    k = np.arange(HALF)[:, None] + 0.5
    m = np.arange(BLOCKS)[None, :]
    eye = np.eye(GROUP)
    phase = 2 * np.pi * k * m / (2 * BLOCKS)
    first = np.stack([np.cos(phase), -np.sin(phase)])
    lhs1 = np.einsum("qkm,st->qskmt", first, eye).reshape(2 * GROUP * HALF, BLOCKS * GROUP)
    last = np.stack([np.cos(phase), -np.sin(phase)]) * (2.0 / PERIOD)
    lhs2 = np.einsum("qkm,st->msqtk", last, eye).reshape(BLOCKS * GROUP, 2 * GROUP * HALF)
    r = np.arange(CHUNK)
    cr = 2 * np.pi * (np.outer(r, r) % CHUNK) / CHUNK
    c, s = np.cos(cr), np.sin(cr)
    fwd = np.block([[c, -s], [s, c]])
    inv = np.block([[c, s], [-s, c]])
    tw = 2 * np.pi * k * r[None, :] / PERIOD
    twist = np.stack([np.cos(tw), -np.sin(tw)]).astype(np.float32)
    return lhs1.astype(bf), lhs2.astype(bf), fwd.astype(bf), inv.astype(bf), twist


def dot(a, b):
    return jnp.dot(a, b, preferred_element_type=F32)


def taps_slice(taps_ref, channels):
    return taps_ref.at[:, :, pl.ds(pl.multiple_of(lax.axis_index("tp") * channels, 128), channels)]


def featurize(x, taps):
    row = lax.broadcasted_iota(jnp.int32, x.shape, 0)
    s0, s1, s2 = taps
    x1 = pltpu.roll(x, 1, 0)
    x2 = pltpu.roll(x, 2, 0)
    feat = s0 * x + s1 * jnp.where(row < 1, 0.0, x1) + s2 * jnp.where(row < 2, 0.0, x2)
    row = row[:8]
    tail = jnp.where(row < 1, s1 * x1[:8], 0.0) + jnp.where(row < 2, s2 * x2[:8], 0.0)
    return feat, tail


def head_block(taps_ref, br_ref, go_ref, send_ref, at):
    cols = pl.ds(at, CB)
    nd = CB // 32
    out = pl.ds(at // 32, nd)
    row8 = lax.broadcasted_iota(jnp.int32, (8, CB), 0)
    feats, tails = [], []
    for b in range(3):
        feat, tail = featurize(
            br_ref[b, :, cols].astype(F32), [taps_ref[b, j : j + 1, cols] for j in range(3)]
        )
        feats.append(feat)
        tails.append(tail)
    query, key, value = feats
    go = go_ref[:, cols].astype(F32)
    send_ref[out, 0:32, :] = (key * value).T.astype(BF16).reshape(nd, 32, CHUNK)
    send_ref[out, 32:64, :] = (go * query).T.astype(BF16).reshape(nd, 32, CHUNK)
    heads = jnp.where(
        row8 < 2,
        query[:8],
        jnp.where(
            row8 < 4,
            pltpu.roll(key[:8], 2, 0),
            jnp.where(row8 < 6, pltpu.roll(value[:8], 4, 0), pltpu.roll(go[:8], 6, 0)),
        ),
    )
    ends = jnp.where(
        row8 < 2,
        tails[0],
        jnp.where(row8 < 4, pltpu.roll(tails[1], 2, 0), pltpu.roll(tails[2], 4, 0)),
    )
    upper = lax.broadcasted_iota(jnp.int32, (8, CB), 1) // GROUP % 2 == 1
    padded = jnp.concatenate(
        [
            jnp.where(upper, 0.0, heads),
            jnp.where(upper, 0.0, ends),
            jnp.where(upper, heads, 0.0),
            jnp.where(upper, ends, 0.0),
            jnp.zeros((CHUNK - 32, CB), F32),
        ],
        axis=0,
    )
    turned = padded.T.reshape(nd, 2, GROUP, CHUNK)
    send_ref[out, 64:80, :] = (turned[:, 0] + turned[:, 1]).astype(BF16)


def head_kernel(
    taps_hbm, br_hbm, go_hbm, send_hbm, taps_ref, br_ref, go_ref, send_ref, taps_sem, in_sem, out_sem
):
    channels = go_ref.shape[1]
    nd = CB // 32
    taps_copy = pltpu.make_async_copy(taps_slice(taps_hbm, channels), taps_ref, taps_sem)
    taps_copy.start()
    loads, stores = [], []
    for i in range(channels // CB):
        cols = pl.ds(i * CB, CB)
        loads.append(
            [
                pltpu.make_async_copy(
                    br_hbm.at[:, :, cols], br_ref.at[:, :, cols], in_sem.at[0, i]
                ),
                pltpu.make_async_copy(go_hbm.at[:, cols], go_ref.at[:, cols], in_sem.at[1, i]),
            ]
        )
        for copy in loads[-1]:
            copy.start()
    taps_copy.wait()
    for i in range(channels // CB):
        for copy in loads[i]:
            copy.wait()
        head_block(taps_ref, br_ref, go_ref, send_ref, i * CB)
        out = pl.ds(i * nd, nd)
        stores.append(pltpu.make_async_copy(send_ref.at[out], send_hbm.at[out], out_sem.at[i]))
        stores[-1].start()
    for copy in stores:
        copy.wait()


def twisted(real, imag, twist_ref, sign):
    shape = real.shape
    real = real.reshape(GROUP, HALF, CHUNK)
    imag = imag.reshape(GROUP, HALF, CHUNK)
    c = twist_ref[0]
    s = twist_ref[1] * sign
    out_r = (real * c - imag * s).astype(BF16).reshape(shape)
    out_i = (real * s + imag * c).astype(BF16).reshape(shape)
    return out_r, out_i


def forward(first, twist_ref, fwd_ref):
    half = GROUP * HALF
    re, im = twisted(first[:half], first[half:], twist_ref, 1.0)
    return dot(jnp.concatenate([re, im], axis=1), fwd_ref[...])


def backward(spectrum, twist_ref, inv_ref):
    value = dot(spectrum, inv_ref[...])
    re, im = twisted(value[:, :CHUNK], value[:, CHUNK:], twist_ref, -1.0)
    return jnp.concatenate([re, im], axis=0)


def filter_kernel(filter_ref, lhs1_ref, fwd_ref, twist_ref, out_ref):
    scale = (BLOCKS * CHUNK) ** -0.5
    for j in range(2):
        rows = filter_ref[GROUP * j : GROUP * (j + 1), :]
        stacked = jnp.concatenate(
            [rows[:, CHUNK * m : CHUNK * (m + 1)] for m in range(BLOCKS)], axis=0
        )
        first = dot(lhs1_ref[...], (stacked * scale).astype(BF16))
        out_ref[j] = forward(first, twist_ref, fwd_ref).astype(BF16)


def middle_kernel(
    recv_ref,
    spec_ref,
    lhs1_ref,
    lhs2_hbm,
    fwd_ref,
    inv_ref,
    twist_ref,
    send_hbm,
    corr_ref,
    lhs2_ref,
    send_ref,
    lhs2_sem,
    out_sem,
):
    lhs2_copy = pltpu.make_async_copy(lhs2_hbm, lhs2_ref, lhs2_sem)
    lhs2_copy.start()
    shape = (BLOCKS, GROUP, CHUNK)
    flat = (BLOCKS * GROUP, CHUNK)
    lane = lax.broadcasted_iota(jnp.int32, (GROUP, CHUNK), 1)
    turn = lambda x, by: pltpu.roll(x, by % CHUNK, 2)
    halo = recv_ref[:, 64:80, :].astype(F32)
    before = jnp.concatenate([jnp.zeros((1, GROUP, CHUNK), F32), halo[:-1]], axis=0)
    feat = halo + turn(before, -8)
    prod = turn(feat, -2) * turn(feat, -4)
    gate = feat * turn(halo, -6)
    spectra = []
    for at, fix in ((0, prod), (32, gate)):
        pair = []
        for j in range(2):
            x = recv_ref[:, at + GROUP * j : at + GROUP * (j + 1), :].astype(F32)
            head = fix if j == 0 else turn(fix, -GROUP)
            pair.append(jnp.where(lane < 2, head, x).astype(BF16).reshape(flat))
        first = dot(lhs1_ref[...], jnp.concatenate(pair, axis=1))
        spectra.append(
            [forward(first[:, CHUNK * j : CHUNK * (j + 1)], twist_ref, fwd_ref) for j in range(2)]
        )
    outs = []
    for j in range(2):
        pr, pi = spectra[0][j][:, :CHUNK], spectra[0][j][:, CHUNK:]
        gr, gi = spectra[1][j][:, :CHUNK], spectra[1][j][:, CHUNK:]
        hr = spec_ref[j, :, :CHUNK].astype(F32)
        hi = spec_ref[j, :, CHUNK:].astype(F32)
        join = lambda re, im: jnp.concatenate([re.astype(BF16), im.astype(BF16)], axis=1)
        corr_ref[j] = join(pr * gr + pi * gi, pr * gi - pi * gr)
        conv = backward(join(hr * pr - hi * pi, hr * pi + hi * pr), twist_ref, inv_ref)
        dzeta = backward(join(hr * gr + hi * gi, hr * gi - hi * gr), twist_ref, inv_ref)
        if j == 0:
            lhs2_copy.wait()
        both = dot(lhs2_ref[...], jnp.concatenate([conv, dzeta], axis=1))
        conv = both[:, :CHUNK].reshape(shape)
        dzeta = both[:, CHUNK:].reshape(shape)
        send_ref[:, GROUP * j : GROUP * (j + 1), :] = conv.astype(BF16)
        send_ref[:, 32 + GROUP * j : 32 + GROUP * (j + 1), :] = dzeta.astype(BF16)
        outs.append((conv, dzeta))
    conv = jnp.where(lane < GROUP, outs[0][0], turn(outs[1][0], GROUP))
    dzeta = jnp.where(lane < GROUP, outs[0][1], turn(outs[1][1], GROUP))
    place = lane % GROUP
    heads = jnp.where(
        place < 2,
        conv * turn(halo, -6),
        jnp.where(place < 4, turn(dzeta, 2) * turn(feat, -2), turn(dzeta, 4) * turn(feat, 2)),
    )
    after = jnp.concatenate([heads[1:], jnp.zeros((1, GROUP, CHUNK), F32)], axis=0)
    send_ref[:, 64:80, :] = jnp.where(place < 8, feat, turn(after, 8)).astype(BF16)
    out = pltpu.make_async_copy(send_ref, send_hbm, out_sem)
    out.start()
    out.wait()


def grad_filter_kernel(
    taps_hbm,
    br_hbm,
    go_hbm,
    corr_ref,
    lhs2_hbm,
    inv_ref,
    twist_ref,
    out_ref,
    taps_ref,
    rows_ref,
    lhs2_ref,
    br_ref,
    sems,
):
    channels = go_hbm.shape[1]
    copies = [
        pltpu.make_async_copy(lhs2_hbm, lhs2_ref, sems.at[0]),
        pltpu.make_async_copy(taps_slice(taps_hbm, channels), taps_ref, sems.at[1]),
        pltpu.make_async_copy(br_hbm.at[1:3], br_ref, sems.at[2]),
        pltpu.make_async_copy(go_hbm, rows_ref.at[2], sems.at[3]),
    ]
    for copy in copies:
        copy.start()
    for copy in copies:
        copy.wait()
    for i in range(channels // CB):
        cols = pl.ds(i * CB, CB)
        for b in range(2):
            taps = [taps_ref[b + 1, j : j + 1, cols] for j in range(3)]
            rows_ref[b, :, cols] = featurize(br_ref[b, :, cols].astype(F32), taps)[0].astype(BF16)
    scale = (BLOCKS * CHUNK) ** -0.5
    stacked = jnp.concatenate(
        [backward(corr_ref[j], twist_ref, inv_ref) for j in range(2)], axis=1
    )
    both = dot(lhs2_ref[...], stacked) * scale
    for j in range(2):
        for m in range(BLOCKS):
            out_ref[GROUP * j : GROUP * (j + 1), CHUNK * m : CHUNK * (m + 1)] = both[
                GROUP * m : GROUP * (m + 1), CHUNK * j : CHUNK * (j + 1)
            ]


def tail_block(taps_ref, rows_ref, recv_ref, out_ref, at):
    cols = pl.ds(at, CB)
    src = pl.ds(at // 32, CB // 32)
    row8 = lax.broadcasted_iota(jnp.int32, (8, CB), 0)
    conv = recv_ref[src, 0:32, :].astype(F32).reshape(CB, CHUNK).T
    dzeta = recv_ref[src, 32:64, :].astype(F32).reshape(CB, CHUNK).T
    halo = recv_ref[src, 64:80, :].astype(F32)
    halo = jnp.concatenate([halo, pltpu.roll(halo, CHUNK - GROUP, 2)], axis=1)
    halo = halo.reshape(CB, CHUNK).T
    heads, nexts = halo[:8], halo[8:16]

    def with_head(b, at):
        value = rows_ref[b, :, cols].astype(F32)
        first = jnp.where(row8 < 2, pltpu.roll(heads, 8 - at, 0), value[:8])
        return jnp.concatenate([first, value[8:]], axis=0)

    key = with_head(0, 2)
    value = with_head(1, 4)
    grads = (rows_ref[2, :, cols].astype(F32) * conv, dzeta * value, dzeta * key)
    for b in range(3):
        d = grads[b]
        s0, s1, s2 = (taps_ref[b, j : j + 1, cols] for j in range(3))
        d1 = pltpu.roll(d, CHUNK - 1, 0)
        d2 = pltpu.roll(d, CHUNK - 2, 0)
        e1 = jnp.where(row8 < 7, d1[-8:], pltpu.roll(nexts, (7 - 2 * b) % 8, 0))
        e2 = jnp.where(row8 < 6, d2[-8:], pltpu.roll(nexts, (6 - 2 * b) % 8, 0))
        d1 = jnp.concatenate([d1[:-8], e1], axis=0)
        d2 = jnp.concatenate([d2[:-8], e2], axis=0)
        out_ref[b, :, cols] = (s0 * d + s1 * d1 + s2 * d2).astype(BF16)


def tail_kernel(taps_ref, rows_ref, recv_ref, out_hbm, out_ref, sem):
    stores = []
    for i in range(out_ref.shape[2] // CB):
        tail_block(taps_ref, rows_ref, recv_ref, out_ref, i * CB)
        cols = pl.ds(i * CB, CB)
        stores.append(
            pltpu.make_async_copy(out_ref.at[:, :, cols], out_hbm.at[:, :, cols], sem.at[i])
        )
        stores[-1].start()
    for copy in stores:
        copy.wait()


def params(mib):
    return pltpu.CompilerParams(vmem_limit_bytes=mib << 20)


def exchange(x):
    return lax.all_to_all(x, "ctx", split_axis=0, concat_axis=0, tiled=True)


def per_device(branches, short_taps, long_filter, grad_out):
    lhs1, lhs2, fwd, inv, twist = (jnp.asarray(t) for t in tables())
    tokens, channels = grad_out.shape
    steps = channels // CB
    half = GROUP * HALF
    hbm = pl.BlockSpec(memory_space=pltpu.HBM)
    vmem = pl.BlockSpec(memory_space=pltpu.VMEM)
    dma = pltpu.SemaphoreType.DMA
    wire = (BLOCKS, ROWS, CHUNK)
    spectral = (2, half, 2 * CHUNK)
    held = lambda x: pltpu.with_memory_space_constraint(x, pltpu.HBM)
    branches, short_taps, grad_out, lhs2 = map(held, (branches, short_taps, grad_out, lhs2))
    send = pl.pallas_call(
        head_kernel,
        in_specs=[hbm, hbm, hbm],
        out_specs=hbm,
        out_shape=pltpu.HBM(wire, BF16),
        scratch_shapes=[
            pltpu.VMEM((3, 3, channels), F32),
            pltpu.VMEM((3, tokens, channels), BF16),
            pltpu.VMEM((tokens, channels), BF16),
            pltpu.VMEM(wire, BF16),
            dma,
            dma((2, steps)),
            dma((steps,)),
        ],
        compiler_params=params(24),
        name="head",
    )(short_taps, branches, grad_out)
    spectrum = pl.pallas_call(
        filter_kernel,
        in_specs=[vmem] * 4,
        out_specs=vmem,
        out_shape=pltpu.VMEM(spectral, BF16),
        compiler_params=params(32),
        name="filter_spectrum",
    )(long_filter, lhs1, fwd, twist)
    recv = exchange(send)
    back, corr = pl.pallas_call(
        middle_kernel,
        in_specs=[vmem, vmem, vmem, hbm, vmem, vmem, vmem],
        out_specs=[hbm, vmem],
        out_shape=[pltpu.HBM(wire, BF16), pltpu.VMEM(spectral, BF16)],
        scratch_shapes=[pltpu.VMEM(lhs2.shape, BF16), pltpu.VMEM(wire, BF16), dma, dma],
        compiler_params=params(32),
        name="middle",
    )(recv, spectrum, lhs1, lhs2, fwd, inv, twist)
    grad_filter, taps, rows = pl.pallas_call(
        grad_filter_kernel,
        in_specs=[hbm, hbm, hbm, vmem, hbm, vmem, vmem],
        out_specs=[vmem, vmem, vmem],
        out_shape=[
            jax.ShapeDtypeStruct(long_filter.shape, F32),
            pltpu.VMEM((3, 3, channels), F32),
            pltpu.VMEM((3, tokens, channels), BF16),
        ],
        scratch_shapes=[
            pltpu.VMEM(lhs2.shape, BF16),
            pltpu.VMEM((2, tokens, channels), BF16),
            dma((4,)),
        ],
        compiler_params=params(32),
        name="grad_filter",
    )(short_taps, branches, grad_out, corr, lhs2, inv, twist)
    returned = exchange(back)
    grads = pl.pallas_call(
        tail_kernel,
        in_specs=[vmem, vmem, vmem],
        out_specs=hbm,
        out_shape=pltpu.HBM(branches.shape, BF16),
        scratch_shapes=[pltpu.VMEM(branches.shape, BF16), dma((steps,))],
        compiler_params=params(24),
        name="tail",
    )(taps, rows, returned)
    return grads, grad_filter


def solution(mesh):
    in_specs = (P(None, "ctx", "tp"), P(), P(("tp", "ctx"), None), P("ctx", "tp"))
    out_specs = (P(None, "ctx", "tp"), P(("tp", "ctx"), None))
    return jax.shard_map(
        per_device, mesh=mesh, in_specs=in_specs, out_specs=out_specs, check_vma=False
    )
```

```python
import functools

import jax
import jax.numpy as jnp
import ml_dtypes
import numpy as np
from jax import lax
from jax.experimental import pallas as pl
from jax.experimental.pallas import tpu as pltpu
from jax.sharding import PartitionSpec as P

F32 = jnp.float32
BF16 = jnp.bfloat16
CHUNK = 128
BLOCKS = 32
GROUP = 8
SPAN = 8
SLOT = 16
HALF = BLOCKS
PERIOD = 2 * BLOCKS * CHUNK
ROWS = 72
CB = 256

ORDER_IN = [i ^ 21 for i in range(BLOCKS)]
ORDER_OUT = [i ^ 21 for i in range(BLOCKS)]
PLACE_IN = [ORDER_IN.index(i) for i in range(BLOCKS)]
PLACE_OUT = [ORDER_OUT.index(i) for i in range(BLOCKS)]


@functools.lru_cache(maxsize=None)
def tables():
    bf = ml_dtypes.bfloat16
    k = np.arange(HALF)[:, None] + 0.5
    m = np.arange(BLOCKS)[None, :]
    eye = np.eye(GROUP)
    phase = 2 * np.pi * k * m / (2 * BLOCKS)
    first = np.stack([np.cos(phase), -np.sin(phase)])
    lhs1 = np.einsum("qkm,st->sqkmt", first[:, :, ORDER_IN], eye).reshape(2 * GROUP * HALF, BLOCKS * GROUP)
    last = np.stack([np.cos(phase), -np.sin(phase)]) * (2.0 / PERIOD)
    lhs2 = np.einsum("qkm,st->mstqk", last[:, :, ORDER_OUT], eye).reshape(BLOCKS * GROUP, 2 * GROUP * HALF)
    r = np.arange(CHUNK)
    cr = 2 * np.pi * (np.outer(r, r) % CHUNK) / CHUNK
    c, s = np.cos(cr), np.sin(cr)
    fwd = np.block([[c, -s], [s, c]])
    inv = np.block([[c, s], [-s, c]])
    tw = 2 * np.pi * k * r[None, :] / PERIOD
    twist = np.stack([np.cos(tw), -np.sin(tw)]).astype(np.float32)
    return lhs1.astype(bf), lhs2.astype(bf), fwd.astype(bf), inv.astype(bf), twist


def take(x, order):
    return jnp.concatenate([x[i : i + 1] for i in order], axis=0)


def dot(a, b):
    return jnp.dot(a, b, preferred_element_type=F32)


def taps_slice(taps_ref, channels):
    return taps_ref.at[:, :, pl.ds(pl.multiple_of(lax.axis_index("tp") * channels, 128), channels)]


def featurize(x, taps):
    row = lax.broadcasted_iota(jnp.int32, x.shape, 0)
    s0, s1, s2 = taps
    x1 = pltpu.roll(x, 1, 0)
    x2 = pltpu.roll(x, 2, 0)
    feat = s0 * x + s1 * jnp.where(row < 1, 0.0, x1) + s2 * jnp.where(row < 2, 0.0, x2)
    row = row[:8]
    tail = jnp.where(row < 1, s1 * x1[:8], 0.0) + jnp.where(row < 2, s2 * x2[:8], 0.0)
    return feat, tail


def head_block(taps_ref, br_ref, go_ref, send_ref, at):
    cols = pl.ds(at, CB)
    nd = CB // 32
    row8 = lax.broadcasted_iota(jnp.int32, (8, CB), 0)
    feats, tails = [], []
    for b in range(3):
        feat, tail = featurize(
            br_ref[b, :, cols].astype(F32), [taps_ref[b, j : j + 1, cols] for j in range(3)]
        )
        feats.append(feat)
        tails.append(tail)
    query, key, value = feats
    go = go_ref[:, cols].astype(F32)
    products = (key * value).astype(BF16).T.reshape(nd, 32, CHUNK)
    gate_grad = (go * query).astype(BF16).T.reshape(nd, 32, CHUNK)
    heads = jnp.where(
        row8 < 2,
        query[:8],
        jnp.where(
            row8 < 4,
            pltpu.roll(key[:8], 2, 0),
            jnp.where(row8 < 6, pltpu.roll(value[:8], 4, 0), pltpu.roll(go[:8], 6, 0)),
        ),
    )
    ends = jnp.where(
        row8 < 2,
        tails[0],
        jnp.where(row8 < 4, pltpu.roll(tails[1], 2, 0), pltpu.roll(tails[2], 4, 0)),
    )
    quarter = lax.broadcasted_iota(jnp.int32, (8, CB), 1) // 8 % 4
    padded = []
    for q in range(4):
        padded += [jnp.where(quarter == q, heads, 0.0), jnp.where(quarter == q, ends, 0.0)]
    padded.append(jnp.zeros((CHUNK - 64, CB), F32))
    terms = jnp.concatenate(padded, axis=0).T.reshape(nd, 4, 8, CHUNK)
    terms = (terms[:, 0] + terms[:, 1] + terms[:, 2] + terms[:, 3]).astype(BF16)
    for n in range(nd):
        place = PLACE_IN[at // 32 + n]
        send_ref[place, 0:32, :] = products[n]
        send_ref[place, 32:64, :] = gate_grad[n]
        send_ref[place, 64:72, :] = terms[n]


def head_kernel(
    taps_hbm, br_hbm, go_hbm, send_hbm, taps_ref, br_ref, go_ref, send_ref, taps_sem, in_sem, out_sem
):
    channels = go_ref.shape[1]
    nd = CB // 32
    taps_copy = pltpu.make_async_copy(taps_slice(taps_hbm, channels), taps_ref, taps_sem)
    taps_copy.start()
    loads, stores = [], []
    for i in range(channels // CB):
        cols = pl.ds(i * CB, CB)
        loads.append(
            [
                pltpu.make_async_copy(
                    br_hbm.at[:, :, cols], br_ref.at[:, :, cols], in_sem.at[0, i]
                ),
                pltpu.make_async_copy(go_hbm.at[:, cols], go_ref.at[:, cols], in_sem.at[1, i]),
            ]
        )
        for copy in loads[-1]:
            copy.start()
    taps_copy.wait()
    for i in range(channels // CB):
        for copy in loads[i]:
            copy.wait()
        head_block(taps_ref, br_ref, go_ref, send_ref, i * CB)
        places = PLACE_IN[i * nd : (i + 1) * nd]
        out = pl.ds(min(places), nd)
        assert max(places) - min(places) == nd - 1
        stores.append(pltpu.make_async_copy(send_ref.at[out], send_hbm.at[out], out_sem.at[i]))
        stores[-1].start()
    for copy in stores:
        copy.wait()


def forward(signals, lhs1_ref, twist_ref, fwd_ref, apply):
    c, s = twist_ref[0], twist_ref[1]
    first = dot(lhs1_ref[...], jnp.concatenate(signals, axis=1))
    turned = []
    for ch in range(GROUP):
        at = 2 * HALF * ch
        for i in range(len(signals)):
            lanes = slice(CHUNK * i, CHUNK * (i + 1))
            re, im = first[at : at + HALF, lanes], first[at + HALF : at + 2 * HALF, lanes]
            pair = [(re * c - im * s).astype(BF16), (re * s + im * c).astype(BF16)]
            turned.append(jnp.concatenate(pair, axis=1))
    step = SPAN * len(signals)
    for at in range(0, len(turned), step):
        spectra = dot(jnp.concatenate(turned[at : at + step], axis=0), fwd_ref[...])
        for n in range(SPAN):
            parts = [
                spectra[HALF * (n * len(signals) + i) :][:HALF] for i in range(len(signals))
            ]
            apply(at // len(signals) + n, parts)


def backward(spectra, lhs2_ref, twist_ref, inv_ref):
    c, s = twist_ref[0], twist_ref[1]
    count = len(spectra[0])
    turned = []
    for at in range(0, GROUP, SPAN):
        flat = [x for channel in spectra[at : at + SPAN] for x in channel]
        value = dot(jnp.concatenate(flat, axis=0), inv_ref[...])
        for n in range(SPAN):
            res, ims = [], []
            for i in range(count):
                part = value[HALF * (n * count + i) :][:HALF]
                re, im = part[:, :CHUNK], part[:, CHUNK:]
                res.append((re * c + im * s).astype(BF16))
                ims.append((im * c - re * s).astype(BF16))
            turned.append(jnp.concatenate(res, axis=1))
            turned.append(jnp.concatenate(ims, axis=1))
    both = dot(lhs2_ref[...], jnp.concatenate(turned, axis=0))
    return [both[:, CHUNK * i : CHUNK * (i + 1)] for i in range(count)]


def filter_kernel(filter_ref, lhs1_ref, fwd_ref, twist_ref, out_ref):
    scale = (BLOCKS * CHUNK) ** -0.5
    for pair in range(2):
        signals = []
        for g in (2 * pair, 2 * pair + 1):
            rows = filter_ref[GROUP * g : GROUP * (g + 1), :] * scale
            stacked = [rows[:, CHUNK * m : CHUNK * (m + 1)] for m in ORDER_IN]
            signals.append(jnp.concatenate(stacked, axis=0).astype(BF16))

        def store(ch, parts):
            rows = slice(HALF * ch, HALF * (ch + 1))
            for i in range(2):
                out_ref[2 * pair + i, rows] = parts[i].astype(BF16)

        forward(signals, lhs1_ref, twist_ref, fwd_ref, store)


def middle_kernel(
    recv_ref,
    spec_ref,
    lhs1_ref,
    lhs2_ref,
    fwd_ref,
    inv_ref,
    twist_ref,
    send_hbm,
    corr_ref,
    send_ref,
    sems,
):
    shape = (BLOCKS, GROUP, CHUNK)
    flat = (BLOCKS * GROUP, CHUNK)
    lane = lax.broadcasted_iota(jnp.int32, (GROUP, CHUNK), 1)
    turn = lambda x, by: pltpu.roll(x, by % CHUNK, 2)
    halo = take(recv_ref[:, 64:72, :].astype(F32), PLACE_IN)
    before = jnp.concatenate([jnp.zeros((1, 8, CHUNK), F32), halo[:-1]], axis=0)
    feat = halo + turn(before, -8)
    prod = take(turn(feat, -2) * turn(feat, -4), ORDER_IN)
    gate = take(feat * turn(halo, -6), ORDER_IN)
    copies, outs, mixes = [], [], []
    join = lambda re, im: jnp.concatenate([re.astype(BF16), im.astype(BF16)], axis=1)
    for j in range(2):
        both = [recv_ref[:, at + 16 * j : at + 16 * (j + 1), :].astype(F32) for at in (0, 32)]
        for h in range(2):
            g = 2 * j + h
            rows = slice(GROUP * h, GROUP * (h + 1))
            signals = []
            for x, fix in zip(both, (prod, gate)):
                fixed = jnp.where(lane < 2, turn(fix, -SLOT * g), x[:, rows])
                signals.append(fixed.reshape(flat).astype(BF16))
            mixed = []

            def mix(ch, parts):
                rows = slice(HALF * ch, HALF * (ch + 1))
                (pr, pi), (gr, gi) = [(x[:, :CHUNK], x[:, CHUNK:]) for x in parts]
                hr = spec_ref[g, rows, :CHUNK].astype(F32)
                hi = spec_ref[g, rows, CHUNK:].astype(F32)
                corr_ref[g, rows] = join(pr * gr + pi * gi, pr * gi - pi * gr)
                mixed.append(
                    [
                        join(hr * pr - hi * pi, hr * pi + hi * pr),
                        join(hr * gr + hi * gi, hr * gi - hi * gr),
                    ]
                )

            forward(signals, lhs1_ref, twist_ref, fwd_ref, mix)
            mixes.append(mixed)
    for j in range(2):
        convs, dzetas = [], []
        for h in range(2):
            conv, dzeta = backward(mixes[2 * j + h], lhs2_ref, twist_ref, inv_ref)
            convs.append(conv.reshape(shape))
            dzetas.append(dzeta.reshape(shape))
        outs.append((convs, dzetas))
        for i in range(2):
            rows = slice(32 * i + 16 * j, 32 * i + 16 * (j + 1))
            send_ref[:, rows, :] = jnp.concatenate(outs[j][i], axis=1).astype(BF16)
            rows = pl.ds(32 * i + 16 * j, 16)
            copies.append(
                pltpu.make_async_copy(send_ref.at[:, rows], send_hbm.at[:, rows], sems.at[i, j])
            )
            copies[-1].start()
    merged = []
    for i in range(2):
        merged.append(outs[0][i][0])
        for g in range(1, 4):
            value = turn(outs[g // 2][i][g % 2], SLOT * g)
            merged[i] = jnp.where(lane < SLOT * g, merged[i], value)
    conv, dzeta = [take(x, PLACE_OUT) for x in merged]
    place = lane % SLOT
    heads = jnp.where(
        place < 2,
        conv * turn(halo, -6),
        jnp.where(place < 4, turn(dzeta, 2) * turn(feat, -2), turn(dzeta, 4) * turn(feat, 2)),
    )
    after = jnp.concatenate([heads[1:], jnp.zeros((1, 8, CHUNK), F32)], axis=0)
    terms = take(jnp.where(place < 8, feat, turn(after, 8)), ORDER_OUT)
    send_ref[:, 64:72, :] = terms.astype(BF16)
    rows = pl.ds(64, 8)
    copies.append(pltpu.make_async_copy(send_ref.at[:, rows], send_hbm.at[:, rows], sems.at[2, 0]))
    copies[-1].start()
    for copy in copies:
        copy.wait()


def grad_filter_kernel(
    taps_hbm,
    br_hbm,
    go_hbm,
    corr_ref,
    lhs2_ref,
    inv_ref,
    twist_ref,
    out_ref,
    taps_ref,
    rows_ref,
    br_ref,
    sems,
):
    channels = go_hbm.shape[1]
    copies = [
        pltpu.make_async_copy(taps_slice(taps_hbm, channels), taps_ref, sems.at[0]),
        pltpu.make_async_copy(br_hbm.at[1:3], br_ref, sems.at[1]),
        pltpu.make_async_copy(go_hbm, rows_ref.at[2], sems.at[2]),
    ]
    for copy in copies:
        copy.start()
    for copy in copies:
        copy.wait()
    for i in range(channels // CB):
        cols = pl.ds(i * CB, CB)
        for b in range(2):
            taps = [taps_ref[b + 1, j : j + 1, cols] for j in range(3)]
            rows_ref[b, :, cols] = featurize(br_ref[b, :, cols].astype(F32), taps)[0].astype(BF16)
    scale = (BLOCKS * CHUNK) ** -0.5
    for pair in range(2):
        spectra = [
            [corr_ref[2 * pair + i, HALF * ch : HALF * (ch + 1)] for i in range(2)]
            for ch in range(GROUP)
        ]
        values = backward(spectra, lhs2_ref, twist_ref, inv_ref)
        for i in range(2):
            at = GROUP * (2 * pair + i)
            for n, m in enumerate(ORDER_OUT):
                out_ref[at : at + GROUP, CHUNK * m : CHUNK * (m + 1)] = (
                    values[i][GROUP * n : GROUP * (n + 1)] * scale
                )


def tail_block(taps_ref, rows_ref, recv_ref, out_ref, at):
    cols = pl.ds(at, CB)
    row8 = lax.broadcasted_iota(jnp.int32, (8, CB), 0)
    places = PLACE_OUT[at // 32 : (at + CB) // 32]
    received = lambda rows: jnp.stack([recv_ref[p, rows, :] for p in places])
    conv = received(slice(0, 32)).reshape(CB, CHUNK).T.astype(F32)
    dzeta = received(slice(32, 64)).reshape(CB, CHUNK).T.astype(F32)
    halo = received(slice(64, 72)).astype(F32)
    turned = [halo] + [pltpu.roll(halo, CHUNK - SLOT * q, 2) for q in range(1, 4)]
    halo = jnp.concatenate(turned, axis=1).reshape(CB, CHUNK).T
    heads, nexts = halo[:8], halo[8:16]

    def with_head(b, at):
        value = rows_ref[b, :, cols].astype(F32)
        first = jnp.where(row8 < 2, pltpu.roll(heads, 8 - at, 0), value[:8])
        return jnp.concatenate([first, value[8:]], axis=0)

    key = with_head(0, 2)
    value = with_head(1, 4)
    grads = (rows_ref[2, :, cols].astype(F32) * conv, dzeta * value, dzeta * key)
    for b in range(3):
        d = grads[b]
        s0, s1, s2 = (taps_ref[b, j : j + 1, cols] for j in range(3))
        d1 = pltpu.roll(d, CHUNK - 1, 0)
        d2 = pltpu.roll(d, CHUNK - 2, 0)
        e1 = jnp.where(row8 < 7, d1[-8:], pltpu.roll(nexts, (7 - 2 * b) % 8, 0))
        e2 = jnp.where(row8 < 6, d2[-8:], pltpu.roll(nexts, (6 - 2 * b) % 8, 0))
        d1 = jnp.concatenate([d1[:-8], e1], axis=0)
        d2 = jnp.concatenate([d2[:-8], e2], axis=0)
        out_ref[b, :, cols] = (s0 * d + s1 * d1 + s2 * d2).astype(BF16)


def tail_kernel(taps_ref, rows_ref, recv_ref, out_hbm, out_ref, sem):
    stores = []
    for i in range(out_ref.shape[2] // CB):
        tail_block(taps_ref, rows_ref, recv_ref, out_ref, i * CB)
        cols = pl.ds(i * CB, CB)
        stores.append(
            pltpu.make_async_copy(out_ref.at[:, :, cols], out_hbm.at[:, :, cols], sem.at[i])
        )
        stores[-1].start()
    for copy in stores:
        copy.wait()


def params(mib):
    return pltpu.CompilerParams(vmem_limit_bytes=mib << 20)


def exchange(x, order):
    return lax.all_to_all(
        x, "ctx", split_axis=0, concat_axis=0, axis_index_groups=[order], tiled=True
    )


def per_device(branches, short_taps, long_filter, grad_out):
    lhs1, lhs2, fwd, inv, twist = (jnp.asarray(t) for t in tables())
    tokens, channels = grad_out.shape
    steps = channels // CB
    half = GROUP * HALF
    hbm = pl.BlockSpec(memory_space=pltpu.HBM)
    vmem = pl.BlockSpec(memory_space=pltpu.VMEM)
    dma = pltpu.SemaphoreType.DMA
    wire = (BLOCKS, ROWS, CHUNK)
    spectral = (32 // GROUP, half, 2 * CHUNK)
    held = lambda x: pltpu.with_memory_space_constraint(x, pltpu.HBM)
    branches, short_taps, grad_out = map(held, (branches, short_taps, grad_out))
    send = pl.pallas_call(
        head_kernel,
        in_specs=[hbm, hbm, hbm],
        out_specs=hbm,
        out_shape=pltpu.HBM(wire, BF16),
        scratch_shapes=[
            pltpu.VMEM((3, 3, channels), F32),
            pltpu.VMEM((3, tokens, channels), BF16),
            pltpu.VMEM((tokens, channels), BF16),
            pltpu.VMEM(wire, BF16),
            dma,
            dma((2, steps)),
            dma((steps,)),
        ],
        compiler_params=params(24),
        name="head",
    )(short_taps, branches, grad_out)
    spectrum = pl.pallas_call(
        filter_kernel,
        in_specs=[vmem] * 4,
        out_specs=vmem,
        out_shape=pltpu.VMEM(spectral, BF16),
        compiler_params=params(32),
        name="filter_spectrum",
    )(long_filter, lhs1, fwd, twist)
    recv = exchange(send, ORDER_IN)
    back, corr = pl.pallas_call(
        middle_kernel,
        in_specs=[vmem] * 7,
        out_specs=[hbm, vmem],
        out_shape=[pltpu.HBM(wire, BF16), pltpu.VMEM(spectral, BF16)],
        scratch_shapes=[pltpu.VMEM(wire, BF16), dma((3, 2))],
        compiler_params=params(32),
        name="middle",
    )(recv, spectrum, lhs1, lhs2, fwd, inv, twist)
    grad_filter, taps, rows = pl.pallas_call(
        grad_filter_kernel,
        in_specs=[hbm, hbm, hbm, vmem, vmem, vmem, vmem],
        out_specs=[vmem, vmem, vmem],
        out_shape=[
            jax.ShapeDtypeStruct(long_filter.shape, F32),
            pltpu.VMEM((3, 3, channels), F32),
            pltpu.VMEM((3, tokens, channels), BF16),
        ],
        scratch_shapes=[
            pltpu.VMEM((2, tokens, channels), BF16),
            dma((3,)),
        ],
        compiler_params=params(32),
        name="grad_filter",
    )(short_taps, branches, grad_out, corr, lhs2, inv, twist)
    returned = exchange(back, ORDER_OUT)
    grads = pl.pallas_call(
        tail_kernel,
        in_specs=[vmem, vmem, vmem],
        out_specs=hbm,
        out_shape=pltpu.HBM(branches.shape, BF16),
        scratch_shapes=[pltpu.VMEM(branches.shape, BF16), dma((steps,))],
        compiler_params=params(24),
        name="tail",
    )(taps, rows, returned)
    return grads, grad_filter


def solution(mesh):
    in_specs = (P(None, "ctx", "tp"), P(), P(("tp", "ctx"), None), P("ctx", "tp"))
    out_specs = (P(None, "ctx", "tp"), P(("tp", "ctx"), None))
    return jax.shard_map(
        per_device, mesh=mesh, in_specs=in_specs, out_specs=out_specs, check_vma=False
    )
```

```python
import functools

import jax
import jax.numpy as jnp
import ml_dtypes
import numpy as np
from jax import lax
from jax.experimental import pallas as pl
from jax.experimental.pallas import tpu as pltpu
from jax.sharding import PartitionSpec as P

F32 = jnp.float32
BF16 = jnp.bfloat16
CHUNK = 128
BLOCKS = 32
GROUP = 8
SLOT = 16
HALF = BLOCKS
PERIOD = 2 * BLOCKS * CHUNK
ROWS = 72
CB = 256


def ctx_order():
    lexical = [8 * z + 2 * y + x for y in range(4) for x in range(2) for z in range(4)]
    return [lexical[13 * j % BLOCKS] ^ 21 for j in range(BLOCKS)]


ORDER_IN = ctx_order()
ORDER_OUT = ctx_order()
PLACE_IN = [ORDER_IN.index(i) for i in range(BLOCKS)]
PLACE_OUT = [ORDER_OUT.index(i) for i in range(BLOCKS)]


@functools.lru_cache(maxsize=None)
def tables():
    bf = ml_dtypes.bfloat16
    k = np.arange(HALF)[:, None] + 0.5
    m = np.arange(BLOCKS)[None, :]
    eye = np.eye(GROUP)
    phase = 2 * np.pi * k * m / (2 * BLOCKS)
    first = np.stack([np.cos(phase), -np.sin(phase)])
    lhs1 = np.einsum("qkm,st->sqkmt", first[:, :, ORDER_IN], eye).reshape(2 * GROUP * HALF, BLOCKS * GROUP)
    last = np.stack([np.cos(phase), -np.sin(phase)]) * (2.0 / PERIOD)
    lhs2 = np.einsum("qkm,st->mstqk", last[:, :, ORDER_OUT], eye).reshape(BLOCKS * GROUP, 2 * GROUP * HALF)
    r = np.arange(CHUNK)
    cr = 2 * np.pi * (np.outer(r, r) % CHUNK) / CHUNK
    c, s = np.cos(cr), np.sin(cr)
    fwd = np.block([[c, -s], [s, c]])
    inv = np.block([[c, s], [-s, c]])
    tw = 2 * np.pi * k * r[None, :] / PERIOD
    twist = np.stack([np.cos(tw), -np.sin(tw)]).astype(np.float32)
    return lhs1.astype(bf), lhs2.astype(bf), fwd.astype(bf), inv.astype(bf), twist


def take(x, order):
    return jnp.concatenate([x[i : i + 1] for i in order], axis=0)


def runs(places):
    found = []
    for p in sorted(places):
        if found and sum(found[-1]) == p:
            found[-1] = (found[-1][0], found[-1][1] + 1)
        else:
            found.append((p, 1))
    return found


def dot(a, b):
    return jnp.dot(a, b, preferred_element_type=F32)


def taps_slice(taps_ref, channels):
    return taps_ref.at[:, :, pl.ds(pl.multiple_of(lax.axis_index("tp") * channels, 128), channels)]


def featurize(x, taps):
    s0, s1, s2 = taps
    x1 = pltpu.roll(x, 1, 0)
    x2 = pltpu.roll(x, 2, 0)
    feat = s0 * x[8:] + s1 * x1[8:] + s2 * x2[8:]
    row = lax.broadcasted_iota(jnp.int32, (8, x.shape[1]), 0)
    one, two = s1 * x1[:8], s2 * x2[:8]
    first = s0 * x[:8] + jnp.where(row < 1, 0.0, one) + jnp.where(row < 2, 0.0, two)
    tail = jnp.where(row < 1, one, 0.0) + jnp.where(row < 2, two, 0.0)
    return jnp.concatenate([first, feat], axis=0), tail


def head_block(taps_ref, rows_ref, send_ref, at):
    cols = pl.ds(at, CB)
    nd = CB // 32
    row8 = lax.broadcasted_iota(jnp.int32, (8, CB), 0)
    feats, tails = [], []
    for b in range(3):
        feat, tail = featurize(
            rows_ref[b, :, cols].astype(F32), [taps_ref[b, j : j + 1, cols] for j in range(3)]
        )
        feats.append(feat)
        tails.append(tail)
    query, key, value = feats
    go = rows_ref[3, :, cols].astype(F32)
    products = (key * value).astype(BF16).T.reshape(nd, 32, CHUNK)
    gate_grad = (go * query).astype(BF16).T.reshape(nd, 32, CHUNK)
    heads = jnp.where(
        row8 < 2,
        query[:8],
        jnp.where(
            row8 < 4,
            pltpu.roll(key[:8], 2, 0),
            jnp.where(row8 < 6, pltpu.roll(value[:8], 4, 0), pltpu.roll(go[:8], 6, 0)),
        ),
    )
    ends = jnp.where(
        row8 < 2,
        tails[0],
        jnp.where(row8 < 4, pltpu.roll(tails[1], 2, 0), pltpu.roll(tails[2], 4, 0)),
    )
    quarter = lax.broadcasted_iota(jnp.int32, (8, CB), 1) // 8 % 4
    padded = []
    for q in range(4):
        padded += [jnp.where(quarter == q, heads, 0.0), jnp.where(quarter == q, ends, 0.0)]
    padded.append(jnp.zeros((CHUNK - 64, CB), F32))
    terms = jnp.concatenate(padded, axis=0).T.reshape(nd, 4, 8, CHUNK)
    terms = (terms[:, 0] + terms[:, 1] + terms[:, 2] + terms[:, 3]).astype(BF16)
    for n in range(nd):
        place = PLACE_IN[at // 32 + n]
        send_ref[place, 0:32, :] = products[n]
        send_ref[place, 32:64, :] = gate_grad[n]
        send_ref[place, 64:72, :] = terms[n]


def head_kernel(
    taps_hbm, br_hbm, go_hbm, send_hbm, taps_ref, rows_ref, send_ref, taps_sem, in_sem, out_sem
):
    channels = rows_ref.shape[2]
    nd = CB // 32
    taps_copy = pltpu.make_async_copy(taps_slice(taps_hbm, channels), taps_ref, taps_sem)
    taps_copy.start()
    blocks = [pl.ds(i * CB, CB) for i in range(channels // CB)]
    for i, cols in enumerate(blocks):
        dst = rows_ref.at[0:3, :, cols]
        pltpu.make_async_copy(br_hbm.at[:, :, cols], dst, in_sem.at[i]).start()
        pltpu.make_async_copy(go_hbm.at[:, cols], rows_ref.at[3, :, cols], in_sem.at[i]).start()
    taps_copy.wait()
    for i, cols in enumerate(blocks):
        both = rows_ref.at[:, :, cols]
        pltpu.make_async_copy(both, both, in_sem.at[i]).wait()
        head_block(taps_ref, rows_ref, send_ref, i * CB)
        for first, length in runs(PLACE_IN[i * nd : (i + 1) * nd]):
            out = pl.ds(first, length)
            pltpu.make_async_copy(send_ref.at[out], send_hbm.at[out], out_sem).start()
    pltpu.make_async_copy(send_ref, send_hbm, out_sem).wait()


def spread(signals, lhs1_ref, twist_ref):
    c, s = twist_ref[0], twist_ref[1]
    first = dot(lhs1_ref[...], jnp.concatenate(signals, axis=1))
    turned = []
    for ch in range(GROUP):
        at = 2 * HALF * ch
        for i in range(len(signals)):
            lanes = slice(CHUNK * i, CHUNK * (i + 1))
            re, im = first[at : at + HALF, lanes], first[at + HALF : at + 2 * HALF, lanes]
            pair = [(re * c - im * s).astype(BF16), (re * s + im * c).astype(BF16)]
            turned.append(jnp.concatenate(pair, axis=1))
    return jnp.concatenate(turned, axis=0)


def forward(signals, lhs1_ref, twist_ref, fwd_ref, apply):
    count = len(signals)
    spectra = dot(spread(signals, lhs1_ref, twist_ref), fwd_ref[...])
    for n in range(GROUP):
        apply(n, [spectra[HALF * (n * count + i) :][:HALF] for i in range(count)])


def gather(value, count, twist_ref):
    c, s = twist_ref[0], twist_ref[1]
    turned = []
    for n in range(GROUP):
        res, ims = [], []
        for i in range(count):
            part = value[HALF * (n * count + i) :][:HALF]
            re, im = part[:, :CHUNK], part[:, CHUNK:]
            res.append((re * c + im * s).astype(BF16))
            ims.append((im * c - re * s).astype(BF16))
        turned.append(jnp.concatenate(res, axis=1))
        turned.append(jnp.concatenate(ims, axis=1))
    return jnp.concatenate(turned, axis=0)


def backward(spectra, lhs2_ref, twist_ref, inv_ref):
    count = len(spectra[0])
    value = dot(jnp.concatenate([x for ch in spectra for x in ch], axis=0), inv_ref[...])
    both = dot(lhs2_ref[...], gather(value, count, twist_ref))
    return [both[:, CHUNK * i : CHUNK * (i + 1)] for i in range(count)]


def filter_kernel(filter_ref, lhs1_ref, fwd_ref, twist_ref, out_ref):
    scale = (BLOCKS * CHUNK) ** -0.5
    for pair in range(2):
        signals = []
        for g in (2 * pair, 2 * pair + 1):
            rows = filter_ref[GROUP * g : GROUP * (g + 1), :] * scale
            stacked = [rows[:, CHUNK * m : CHUNK * (m + 1)] for m in ORDER_IN]
            signals.append(jnp.concatenate(stacked, axis=0).astype(BF16))

        def store(ch, parts):
            rows = slice(HALF * ch, HALF * (ch + 1))
            for i in range(2):
                out_ref[2 * pair + i, rows] = parts[i].astype(BF16)

        forward(signals, lhs1_ref, twist_ref, fwd_ref, store)


def middle_kernel(
    recv_ref,
    spec_ref,
    lhs1_ref,
    lhs2_ref,
    fwd_ref,
    inv_ref,
    twist_ref,
    send_hbm,
    corr_ref,
    send_ref,
    sem,
):
    shape = (BLOCKS, GROUP, CHUNK)
    flat = (BLOCKS * GROUP, CHUNK)
    lane = lax.broadcasted_iota(jnp.int32, (GROUP, CHUNK), 1)
    turn = lambda x, by: pltpu.roll(x, by % CHUNK, 2)
    halo = take(recv_ref[:, 64:72, :].astype(F32), PLACE_IN)
    before = jnp.concatenate([jnp.zeros((1, 8, CHUNK), F32), halo[:-1]], axis=0)
    feat = halo + turn(before, -8)
    prod = take(turn(feat, -2) * turn(feat, -4), ORDER_IN)
    gate = take(feat * turn(halo, -6), ORDER_IN)
    outs, mixes, spreads = [], [], []
    join = lambda re, im: jnp.concatenate([re.astype(BF16), im.astype(BF16)], axis=1)
    for j in range(2):
        both = [recv_ref[:, at + 16 * j : at + 16 * (j + 1), :].astype(F32) for at in (0, 32)]
        for h in range(2):
            g = 2 * j + h
            rows = slice(GROUP * h, GROUP * (h + 1))
            signals = []
            for x, fix in zip(both, (prod, gate)):
                fixed = jnp.where(lane < 2, turn(fix, -SLOT * g), x[:, rows])
                signals.append(fixed.reshape(flat).astype(BF16))
            spreads.append(spread(signals, lhs1_ref, twist_ref))
    size = 2 * GROUP * HALF
    everything = dot(jnp.concatenate(spreads, axis=0), fwd_ref[...])
    for g in range(4):
        spectra = everything[size * g : size * (g + 1)]
        mixed = []
        for ch in range(GROUP):
            at = 2 * HALF * ch
            parts = (spectra[at : at + HALF], spectra[at + HALF : at + 2 * HALF])
            (pr, pi), (gr, gi) = [(x[:, :CHUNK], x[:, CHUNK:]) for x in parts]
            rows = slice(HALF * ch, HALF * (ch + 1))
            hr = spec_ref[g, rows, :CHUNK].astype(F32)
            hi = spec_ref[g, rows, CHUNK:].astype(F32)
            corr_ref[g, rows] = join(pr * gr + pi * gi, pr * gi - pi * gr)
            mixed.append(join(hr * pr - hi * pi, hr * pi + hi * pr))
            mixed.append(join(hr * gr + hi * gi, hr * gi - hi * gr))
        mixes.append(jnp.concatenate(mixed, axis=0))
    everything = dot(jnp.concatenate(mixes, axis=0), inv_ref[...])
    gathers = [gather(everything[size * g : size * (g + 1)], 2, twist_ref) for g in range(4)]
    for j in range(2):
        convs, dzetas = [], []
        for h in range(2):
            value = dot(lhs2_ref[...], gathers[2 * j + h])
            convs.append(value[:, :CHUNK].reshape(shape))
            dzetas.append(value[:, CHUNK:].reshape(shape))
        outs.append((convs, dzetas))
        for i in range(2):
            rows = slice(32 * i + 16 * j, 32 * i + 16 * (j + 1))
            send_ref[:, rows, :] = jnp.concatenate(outs[j][i], axis=1).astype(BF16)
            rows = pl.ds(32 * i + 16 * j, 16)
            pltpu.make_async_copy(send_ref.at[:, rows], send_hbm.at[:, rows], sem).start()
    merged = []
    for i in range(2):
        merged.append(outs[0][i][0])
        for g in range(1, 4):
            value = turn(outs[g // 2][i][g % 2], SLOT * g)
            merged[i] = jnp.where(lane < SLOT * g, merged[i], value)
    conv, dzeta = [take(x, PLACE_OUT) for x in merged]
    place = lane % SLOT
    heads = jnp.where(
        place < 2,
        conv * turn(halo, -6),
        jnp.where(place < 4, turn(dzeta, 2) * turn(feat, -2), turn(dzeta, 4) * turn(feat, 2)),
    )
    after = jnp.concatenate([heads[1:], jnp.zeros((1, 8, CHUNK), F32)], axis=0)
    terms = take(jnp.where(place < 8, feat, turn(after, 8)), ORDER_OUT)
    send_ref[:, 64:72, :] = terms.astype(BF16)
    rows = pl.ds(64, 8)
    pltpu.make_async_copy(send_ref.at[:, rows], send_hbm.at[:, rows], sem).start()
    pltpu.make_async_copy(send_ref, send_hbm, sem).wait()


def grad_filter_kernel(
    taps_hbm,
    br_hbm,
    go_hbm,
    corr_ref,
    lhs2_ref,
    inv_ref,
    twist_ref,
    out_ref,
    taps_ref,
    rows_ref,
    br_ref,
    sems,
):
    channels = go_hbm.shape[1]
    copies = [
        pltpu.make_async_copy(taps_slice(taps_hbm, channels), taps_ref, sems.at[0]),
        pltpu.make_async_copy(br_hbm.at[1:3], br_ref, sems.at[1]),
        pltpu.make_async_copy(go_hbm, rows_ref.at[2], sems.at[2]),
    ]
    for copy in copies:
        copy.start()
    for copy in copies:
        copy.wait()
    for i in range(channels // CB):
        cols = pl.ds(i * CB, CB)
        for b in range(2):
            taps = [taps_ref[b + 1, j : j + 1, cols] for j in range(3)]
            rows_ref[b, :, cols] = featurize(br_ref[b, :, cols].astype(F32), taps)[0].astype(BF16)
    scale = (BLOCKS * CHUNK) ** -0.5
    for pair in range(2):
        spectra = [
            [corr_ref[2 * pair + i, HALF * ch : HALF * (ch + 1)] for i in range(2)]
            for ch in range(GROUP)
        ]
        values = backward(spectra, lhs2_ref, twist_ref, inv_ref)
        for i in range(2):
            at = GROUP * (2 * pair + i)
            for n, m in enumerate(ORDER_OUT):
                out_ref[at : at + GROUP, CHUNK * m : CHUNK * (m + 1)] = (
                    values[i][GROUP * n : GROUP * (n + 1)] * scale
                )


def tail_block(taps_ref, rows_ref, recv_ref, out_ref, at):
    cols = pl.ds(at, CB)
    row8 = lax.broadcasted_iota(jnp.int32, (8, CB), 0)
    places = PLACE_OUT[at // 32 : (at + CB) // 32]
    received = lambda rows: jnp.stack([recv_ref[p, rows, :] for p in places])
    conv = received(slice(0, 32)).reshape(CB, CHUNK).T.astype(F32)
    dzeta = received(slice(32, 64)).reshape(CB, CHUNK).T.astype(F32)
    halo = received(slice(64, 72)).astype(F32)
    turned = [halo] + [pltpu.roll(halo, CHUNK - SLOT * q, 2) for q in range(1, 4)]
    halo = jnp.concatenate(turned, axis=1).reshape(CB, CHUNK).T
    heads, nexts = halo[:8], halo[8:16]

    def with_head(b, at):
        value = rows_ref[b, :, cols].astype(F32)
        first = jnp.where(row8 < 2, pltpu.roll(heads, 8 - at, 0), value[:8])
        return jnp.concatenate([first, value[8:]], axis=0)

    key = with_head(0, 2)
    value = with_head(1, 4)
    grads = (rows_ref[2, :, cols].astype(F32) * conv, dzeta * value, dzeta * key)
    for b in range(3):
        d = grads[b]
        s0, s1, s2 = (taps_ref[b, j : j + 1, cols] for j in range(3))
        d1 = pltpu.roll(d, CHUNK - 1, 0)
        d2 = pltpu.roll(d, CHUNK - 2, 0)
        e1 = jnp.where(row8 < 7, d1[-8:], pltpu.roll(nexts, (7 - 2 * b) % 8, 0))
        e2 = jnp.where(row8 < 6, d2[-8:], pltpu.roll(nexts, (6 - 2 * b) % 8, 0))
        d1 = jnp.concatenate([d1[:-8], e1], axis=0)
        d2 = jnp.concatenate([d2[:-8], e2], axis=0)
        out_ref[b, :, cols] = (s0 * d + s1 * d1 + s2 * d2).astype(BF16)


def tail_kernel(taps_ref, rows_ref, recv_ref, out_hbm, out_ref, sem):
    for i in range(out_ref.shape[2] // CB):
        tail_block(taps_ref, rows_ref, recv_ref, out_ref, i * CB)
        cols = pl.ds(i * CB, CB)
        pltpu.make_async_copy(out_ref.at[:, :, cols], out_hbm.at[:, :, cols], sem).start()
    pltpu.make_async_copy(out_ref, out_hbm, sem).wait()


def params(mib):
    return pltpu.CompilerParams(vmem_limit_bytes=mib << 20)


def exchange(x, order):
    return lax.all_to_all(
        x, "ctx", split_axis=0, concat_axis=0, axis_index_groups=[order], tiled=True
    )


def per_device(branches, short_taps, long_filter, grad_out):
    lhs1, lhs2, fwd, inv, twist = (jnp.asarray(t) for t in tables())
    tokens, channels = grad_out.shape
    steps = channels // CB
    half = GROUP * HALF
    hbm = pl.BlockSpec(memory_space=pltpu.HBM)
    vmem = pl.BlockSpec(memory_space=pltpu.VMEM)
    dma = pltpu.SemaphoreType.DMA
    wire = (BLOCKS, ROWS, CHUNK)
    spectral = (32 // GROUP, half, 2 * CHUNK)
    held = lambda x: pltpu.with_memory_space_constraint(x, pltpu.HBM)
    branches, short_taps, grad_out = map(held, (branches, short_taps, grad_out))
    send = pl.pallas_call(
        head_kernel,
        in_specs=[hbm, hbm, hbm],
        out_specs=hbm,
        out_shape=pltpu.HBM(wire, BF16),
        scratch_shapes=[
            pltpu.VMEM((3, 3, channels), F32),
            pltpu.VMEM((4, tokens, channels), BF16),
            pltpu.VMEM(wire, BF16),
            dma,
            dma((steps,)),
            dma,
        ],
        compiler_params=params(24),
        name="head",
    )(short_taps, branches, grad_out)
    spectrum = pl.pallas_call(
        filter_kernel,
        in_specs=[vmem] * 4,
        out_specs=vmem,
        out_shape=pltpu.VMEM(spectral, BF16),
        compiler_params=params(32),
        name="filter_spectrum",
    )(long_filter, lhs1, fwd, twist)
    recv = exchange(send, ORDER_IN)
    back, corr = pl.pallas_call(
        middle_kernel,
        in_specs=[vmem] * 7,
        out_specs=[hbm, vmem],
        out_shape=[pltpu.HBM(wire, BF16), pltpu.VMEM(spectral, BF16)],
        scratch_shapes=[pltpu.VMEM(wire, BF16), dma],
        compiler_params=params(32),
        name="middle",
    )(recv, spectrum, lhs1, lhs2, fwd, inv, twist)
    grad_filter, taps, rows = pl.pallas_call(
        grad_filter_kernel,
        in_specs=[hbm, hbm, hbm, vmem, vmem, vmem, vmem],
        out_specs=[vmem, vmem, vmem],
        out_shape=[
            jax.ShapeDtypeStruct(long_filter.shape, F32),
            pltpu.VMEM((3, 3, channels), F32),
            pltpu.VMEM((3, tokens, channels), BF16),
        ],
        scratch_shapes=[
            pltpu.VMEM((2, tokens, channels), BF16),
            dma((3,)),
        ],
        compiler_params=params(32),
        name="grad_filter",
    )(short_taps, branches, grad_out, corr, lhs2, inv, twist)
    returned = exchange(back, ORDER_OUT)
    grads = pl.pallas_call(
        tail_kernel,
        in_specs=[vmem, vmem, vmem],
        out_specs=hbm,
        out_shape=pltpu.HBM(branches.shape, BF16),
        scratch_shapes=[pltpu.VMEM(branches.shape, BF16), dma],
        compiler_params=params(24),
        name="tail",
    )(taps, rows, returned)
    return grads, grad_filter


def solution(mesh):
    in_specs = (P(None, "ctx", "tp"), P(), P(("tp", "ctx"), None), P("ctx", "tp"))
    out_specs = (P(None, "ctx", "tp"), P(("tp", "ctx"), None))
    return jax.shard_map(
        per_device, mesh=mesh, in_specs=in_specs, out_specs=out_specs, check_vma=False
    )
```

```python
import functools

import jax
import jax.numpy as jnp
import ml_dtypes
import numpy as np
from jax import lax
from jax.experimental import pallas as pl
from jax.experimental.pallas import tpu as pltpu
from jax.sharding import PartitionSpec as P

F32 = jnp.float32
BF16 = jnp.bfloat16
CHUNK = 128
BLOCKS = 32
GROUP = 8
SLOT = 16
HALF = BLOCKS
PERIOD = 2 * BLOCKS * CHUNK
ROWS = 72
CB = 256
KB = 128


def ctx_order():
    lexical = [8 * z + 2 * y + x for y in range(4) for x in range(2) for z in range(4)]
    return [lexical[13 * j % BLOCKS] ^ 21 for j in range(BLOCKS)]


ORDER_IN = ctx_order()
ORDER_OUT = ctx_order()
PLACE_IN = [ORDER_IN.index(i) for i in range(BLOCKS)]
PLACE_OUT = [ORDER_OUT.index(i) for i in range(BLOCKS)]


@functools.lru_cache(maxsize=None)
def tables():
    bf = ml_dtypes.bfloat16
    k = np.arange(HALF)[:, None] + 0.5
    m = np.arange(BLOCKS)[None, :]
    eye = np.eye(GROUP)
    phase = 2 * np.pi * k * m / (2 * BLOCKS)
    first = np.stack([np.cos(phase), -np.sin(phase)])
    lhs1 = np.einsum("qkm,st->sqkmt", first[:, :, ORDER_IN], eye).reshape(2 * GROUP * HALF, BLOCKS * GROUP)
    last = np.stack([np.cos(phase), -np.sin(phase)]) * (2.0 / PERIOD)
    lhs2 = np.einsum("qkm,st->mstqk", last[:, :, ORDER_OUT], eye).reshape(BLOCKS * GROUP, 2 * GROUP * HALF)
    r = np.arange(CHUNK)
    cr = 2 * np.pi * (np.outer(r, r) % CHUNK) / CHUNK
    c, s = np.cos(cr), np.sin(cr)
    fwd = np.block([[c, -s], [s, c]])
    inv = np.block([[c, s], [-s, c]])
    tw = 2 * np.pi * k * r[None, :] / PERIOD
    twist = np.stack([np.cos(tw), -np.sin(tw)]).astype(np.float32)
    return lhs1.astype(bf), lhs2.astype(bf), fwd.astype(bf), inv.astype(bf), twist


def take(x, order):
    return jnp.concatenate([x[i : i + 1] for i in order], axis=0)


def runs(places):
    found = []
    for p in sorted(places):
        if found and sum(found[-1]) == p:
            found[-1] = (found[-1][0], found[-1][1] + 1)
        else:
            found.append((p, 1))
    return found


def dot(a, b):
    return jnp.dot(a, b, preferred_element_type=F32)


def taps_slice(taps_ref, channels):
    return taps_ref.at[:, :, pl.ds(pl.multiple_of(lax.axis_index("tp") * channels, 128), channels)]


def featurize(x, taps):
    s0, s1, s2 = taps
    x1 = pltpu.roll(x, 1, 0)
    x2 = pltpu.roll(x, 2, 0)
    feat = s0 * x[8:] + s1 * x1[8:] + s2 * x2[8:]
    row = lax.broadcasted_iota(jnp.int32, (8, x.shape[1]), 0)
    one, two = s1 * x1[:8], s2 * x2[:8]
    first = s0 * x[:8] + jnp.where(row < 1, 0.0, one) + jnp.where(row < 2, 0.0, two)
    tail = jnp.where(row < 1, one, 0.0) + jnp.where(row < 2, two, 0.0)
    return jnp.concatenate([first, feat], axis=0), tail


def head_feat(taps_ref, rows_ref, b, cols):
    taps = [taps_ref[b, j : j + 1, cols] for j in range(3)]
    return featurize(rows_ref[b, :, cols].astype(F32), taps)


def head_store(send_ref, at, rows, value):
    value = value.astype(BF16).T.reshape(KB // 32, 32, CHUNK)
    for n in range(KB // 32):
        send_ref[PLACE_IN[at // 32 + n], rows, :] = value[n]


def head_products(taps_ref, rows_ref, terms_ref, send_ref, at):
    cols = pl.ds(at, KB)
    key, key_tail = head_feat(taps_ref, rows_ref, 1, cols)
    value, value_tail = head_feat(taps_ref, rows_ref, 2, cols)
    head_store(send_ref, at, slice(0, 32), key * value)
    row8 = lax.broadcasted_iota(jnp.int32, (8, KB), 0)
    for i, (k, v) in enumerate(((key[:8], value[:8]), (key_tail, value_tail))):
        terms_ref[i, :, cols] = jnp.where(row8 < 4, pltpu.roll(k, 2, 0), pltpu.roll(v, 4, 0))


def head_gate_grad(taps_ref, rows_ref, terms_ref, send_ref, at):
    cols = pl.ds(at, KB)
    query, query_tail = head_feat(taps_ref, rows_ref, 0, cols)
    go = rows_ref[3, :, cols].astype(F32)
    head_store(send_ref, at, slice(32, 64), go * query)
    row8 = lax.broadcasted_iota(jnp.int32, (8, KB), 0)
    heads = jnp.where(row8 < 6, terms_ref[0, :, cols], pltpu.roll(go[:8], 6, 0))
    heads = jnp.where(row8 < 2, query[:8], heads)
    ends = jnp.where(row8 < 2, query_tail, terms_ref[1, :, cols])
    quarter = lax.broadcasted_iota(jnp.int32, (8, KB), 1) // 8 % 4
    padded = []
    for q in range(4):
        padded += [jnp.where(quarter == q, heads, 0.0), jnp.where(quarter == q, ends, 0.0)]
    padded.append(jnp.zeros((CHUNK - 64, KB), F32))
    terms = jnp.concatenate(padded, axis=0).T.reshape(KB // 32, 4, 8, CHUNK)
    terms = (terms[:, 0] + terms[:, 1] + terms[:, 2] + terms[:, 3]).astype(BF16)
    for n in range(KB // 32):
        send_ref[PLACE_IN[at // 32 + n], 64:72, :] = terms[n]


def head_kernel(
    taps_hbm,
    br_hbm,
    go_hbm,
    send_hbm,
    taps_ref,
    rows_ref,
    terms_ref,
    send_ref,
    taps_sem,
    in_sem,
    out_sem,
):
    channels = rows_ref.shape[2]
    taps_copy = pltpu.make_async_copy(taps_slice(taps_hbm, channels), taps_ref, taps_sem)
    pair_copy = pltpu.make_async_copy(br_hbm.at[1:3], rows_ref.at[1:3], in_sem.at[0])
    query_copy = pltpu.make_async_copy(br_hbm.at[0], rows_ref.at[0], in_sem.at[1])
    go_copy = pltpu.make_async_copy(go_hbm, rows_ref.at[3], in_sem.at[2])
    for copy in (taps_copy, pair_copy, query_copy, go_copy):
        copy.start()
    taps_copy.wait()
    pair_copy.wait()
    for at in range(0, channels, KB):
        head_products(taps_ref, rows_ref, terms_ref, send_ref, at)
    query_copy.wait()
    go_copy.wait()
    for at in range(0, channels, KB):
        head_gate_grad(taps_ref, rows_ref, terms_ref, send_ref, at)
        for first, length in runs(PLACE_IN[at // 32 : (at + KB) // 32]):
            out = pl.ds(first, length)
            pltpu.make_async_copy(send_ref.at[out], send_hbm.at[out], out_sem).start()
    pltpu.make_async_copy(send_ref, send_hbm, out_sem).wait()


def spread(signals, lhs1_ref, twist_ref):
    c, s = twist_ref[0], twist_ref[1]
    first = dot(lhs1_ref[...], jnp.concatenate(signals, axis=1))
    turned = []
    for ch in range(GROUP):
        at = 2 * HALF * ch
        for i in range(len(signals)):
            lanes = slice(CHUNK * i, CHUNK * (i + 1))
            re, im = first[at : at + HALF, lanes], first[at + HALF : at + 2 * HALF, lanes]
            pair = [(re * c - im * s).astype(BF16), (re * s + im * c).astype(BF16)]
            turned.append(jnp.concatenate(pair, axis=1))
    return jnp.concatenate(turned, axis=0)


def forward(signals, lhs1_ref, twist_ref, fwd_ref, apply):
    count = len(signals)
    spectra = dot(spread(signals, lhs1_ref, twist_ref), fwd_ref[...])
    for n in range(GROUP):
        apply(n, [spectra[HALF * (n * count + i) :][:HALF] for i in range(count)])


def gather(value, count, twist_ref):
    c, s = twist_ref[0], twist_ref[1]
    turned = []
    for n in range(GROUP):
        res, ims = [], []
        for i in range(count):
            part = value[HALF * (n * count + i) :][:HALF]
            re, im = part[:, :CHUNK], part[:, CHUNK:]
            res.append((re * c + im * s).astype(BF16))
            ims.append((im * c - re * s).astype(BF16))
        turned.append(jnp.concatenate(res, axis=1))
        turned.append(jnp.concatenate(ims, axis=1))
    return jnp.concatenate(turned, axis=0)


def backward(spectra, lhs2_ref, twist_ref, inv_ref):
    count = len(spectra[0])
    value = dot(jnp.concatenate([x for ch in spectra for x in ch], axis=0), inv_ref[...])
    both = dot(lhs2_ref[...], gather(value, count, twist_ref))
    return [both[:, CHUNK * i : CHUNK * (i + 1)] for i in range(count)]


def filter_kernel(filter_ref, lhs1_ref, fwd_ref, twist_ref, out_ref):
    scale = (BLOCKS * CHUNK) ** -0.5
    for pair in range(2):
        signals = []
        for g in (2 * pair, 2 * pair + 1):
            rows = filter_ref[GROUP * g : GROUP * (g + 1), :] * scale
            stacked = [rows[:, CHUNK * m : CHUNK * (m + 1)] for m in ORDER_IN]
            signals.append(jnp.concatenate(stacked, axis=0).astype(BF16))

        def store(ch, parts):
            rows = slice(HALF * ch, HALF * (ch + 1))
            for i in range(2):
                out_ref[2 * pair + i, rows] = parts[i].astype(BF16)

        forward(signals, lhs1_ref, twist_ref, fwd_ref, store)


def middle_kernel(
    recv_ref,
    spec_ref,
    lhs1_ref,
    lhs2_ref,
    fwd_ref,
    inv_ref,
    twist_ref,
    send_hbm,
    corr_ref,
    send_ref,
    sem,
):
    shape = (BLOCKS, GROUP, CHUNK)
    flat = (BLOCKS * GROUP, CHUNK)
    lane = lax.broadcasted_iota(jnp.int32, (GROUP, CHUNK), 1)
    turn = lambda x, by: pltpu.roll(x, by % CHUNK, 2)
    halo = take(recv_ref[:, 64:72, :].astype(F32), PLACE_IN)
    before = jnp.concatenate([jnp.zeros((1, 8, CHUNK), F32), halo[:-1]], axis=0)
    feat = halo + turn(before, -8)
    prod = take(turn(feat, -2) * turn(feat, -4), ORDER_IN)
    gate = take(feat * turn(halo, -6), ORDER_IN)
    outs, mixes, spreads = [], [], []
    join = lambda re, im: jnp.concatenate([re.astype(BF16), im.astype(BF16)], axis=1)
    for j in range(2):
        both = [recv_ref[:, at + 16 * j : at + 16 * (j + 1), :].astype(F32) for at in (0, 32)]
        for h in range(2):
            g = 2 * j + h
            rows = slice(GROUP * h, GROUP * (h + 1))
            signals = []
            for x, fix in zip(both, (prod, gate)):
                fixed = jnp.where(lane < 2, turn(fix, -SLOT * g), x[:, rows])
                signals.append(fixed.reshape(flat).astype(BF16))
            spreads.append(spread(signals, lhs1_ref, twist_ref))
    size = 2 * GROUP * HALF
    everything = dot(jnp.concatenate(spreads, axis=0), fwd_ref[...])
    for g in range(4):
        spectra = everything[size * g : size * (g + 1)]
        mixed = []
        for ch in range(GROUP):
            at = 2 * HALF * ch
            parts = (spectra[at : at + HALF], spectra[at + HALF : at + 2 * HALF])
            (pr, pi), (gr, gi) = [(x[:, :CHUNK], x[:, CHUNK:]) for x in parts]
            rows = slice(HALF * ch, HALF * (ch + 1))
            hr = spec_ref[g, rows, :CHUNK].astype(F32)
            hi = spec_ref[g, rows, CHUNK:].astype(F32)
            corr_ref[g, rows] = join(pr * gr + pi * gi, pr * gi - pi * gr)
            mixed.append(join(hr * pr - hi * pi, hr * pi + hi * pr))
            mixed.append(join(hr * gr + hi * gi, hr * gi - hi * gr))
        mixes.append(jnp.concatenate(mixed, axis=0))
    everything = dot(jnp.concatenate(mixes, axis=0), inv_ref[...])
    gathers = [gather(everything[size * g : size * (g + 1)], 2, twist_ref) for g in range(4)]
    for j in range(2):
        convs, dzetas = [], []
        for h in range(2):
            value = dot(lhs2_ref[...], gathers[2 * j + h])
            convs.append(value[:, :CHUNK].reshape(shape))
            dzetas.append(value[:, CHUNK:].reshape(shape))
        outs.append((convs, dzetas))
        for i in range(2):
            rows = slice(32 * i + 16 * j, 32 * i + 16 * (j + 1))
            send_ref[:, rows, :] = jnp.concatenate(outs[j][i], axis=1).astype(BF16)
            rows = pl.ds(32 * i + 16 * j, 16)
            pltpu.make_async_copy(send_ref.at[:, rows], send_hbm.at[:, rows], sem).start()
    merged = []
    for i in range(2):
        merged.append(outs[0][i][0])
        for g in range(1, 4):
            value = turn(outs[g // 2][i][g % 2], SLOT * g)
            merged[i] = jnp.where(lane < SLOT * g, merged[i], value)
    conv, dzeta = [take(x, PLACE_OUT) for x in merged]
    place = lane % SLOT
    heads = jnp.where(
        place < 2,
        conv * turn(halo, -6),
        jnp.where(place < 4, turn(dzeta, 2) * turn(feat, -2), turn(dzeta, 4) * turn(feat, 2)),
    )
    after = jnp.concatenate([heads[1:], jnp.zeros((1, 8, CHUNK), F32)], axis=0)
    terms = take(jnp.where(place < 8, feat, turn(after, 8)), ORDER_OUT)
    send_ref[:, 64:72, :] = terms.astype(BF16)
    rows = pl.ds(64, 8)
    pltpu.make_async_copy(send_ref.at[:, rows], send_hbm.at[:, rows], sem).start()
    pltpu.make_async_copy(send_ref, send_hbm, sem).wait()


def grad_filter_kernel(
    taps_hbm,
    br_hbm,
    go_hbm,
    corr_ref,
    lhs2_ref,
    inv_ref,
    twist_ref,
    out_ref,
    taps_ref,
    rows_ref,
    br_ref,
    sems,
):
    channels = go_hbm.shape[1]
    copies = [
        pltpu.make_async_copy(taps_slice(taps_hbm, channels), taps_ref, sems.at[0]),
        pltpu.make_async_copy(br_hbm.at[1:3], br_ref, sems.at[1]),
        pltpu.make_async_copy(go_hbm, rows_ref.at[2], sems.at[2]),
    ]
    for copy in copies:
        copy.start()
    for copy in copies:
        copy.wait()
    for i in range(channels // CB):
        cols = pl.ds(i * CB, CB)
        for b in range(2):
            taps = [taps_ref[b + 1, j : j + 1, cols] for j in range(3)]
            rows_ref[b, :, cols] = featurize(br_ref[b, :, cols].astype(F32), taps)[0].astype(BF16)
    scale = (BLOCKS * CHUNK) ** -0.5
    for pair in range(2):
        spectra = [
            [corr_ref[2 * pair + i, HALF * ch : HALF * (ch + 1)] for i in range(2)]
            for ch in range(GROUP)
        ]
        values = backward(spectra, lhs2_ref, twist_ref, inv_ref)
        for i in range(2):
            at = GROUP * (2 * pair + i)
            for n, m in enumerate(ORDER_OUT):
                out_ref[at : at + GROUP, CHUNK * m : CHUNK * (m + 1)] = (
                    values[i][GROUP * n : GROUP * (n + 1)] * scale
                )


def tail_block(taps_ref, rows_ref, recv_ref, out_ref, at):
    cols = pl.ds(at, CB)
    row8 = lax.broadcasted_iota(jnp.int32, (8, CB), 0)
    places = PLACE_OUT[at // 32 : (at + CB) // 32]
    received = lambda rows: jnp.stack([recv_ref[p, rows, :] for p in places])
    conv = received(slice(0, 32)).reshape(CB, CHUNK).T.astype(F32)
    dzeta = received(slice(32, 64)).reshape(CB, CHUNK).T.astype(F32)
    halo = received(slice(64, 72)).astype(F32)
    turned = [halo] + [pltpu.roll(halo, CHUNK - SLOT * q, 2) for q in range(1, 4)]
    halo = jnp.concatenate(turned, axis=1).reshape(CB, CHUNK).T
    heads, nexts = halo[:8], halo[8:16]

    def with_head(b, at):
        value = rows_ref[b, :, cols].astype(F32)
        first = jnp.where(row8 < 2, pltpu.roll(heads, 8 - at, 0), value[:8])
        return jnp.concatenate([first, value[8:]], axis=0)

    key = with_head(0, 2)
    value = with_head(1, 4)
    grads = (rows_ref[2, :, cols].astype(F32) * conv, dzeta * value, dzeta * key)
    for b in range(3):
        d = grads[b]
        s0, s1, s2 = (taps_ref[b, j : j + 1, cols] for j in range(3))
        d1 = pltpu.roll(d, CHUNK - 1, 0)
        d2 = pltpu.roll(d, CHUNK - 2, 0)
        e1 = jnp.where(row8 < 7, d1[-8:], pltpu.roll(nexts, (7 - 2 * b) % 8, 0))
        e2 = jnp.where(row8 < 6, d2[-8:], pltpu.roll(nexts, (6 - 2 * b) % 8, 0))
        d1 = jnp.concatenate([d1[:-8], e1], axis=0)
        d2 = jnp.concatenate([d2[:-8], e2], axis=0)
        out_ref[b, :, cols] = (s0 * d + s1 * d1 + s2 * d2).astype(BF16)


def tail_kernel(taps_ref, rows_ref, recv_ref, out_hbm, out_ref, sem):
    for i in range(out_ref.shape[2] // CB):
        tail_block(taps_ref, rows_ref, recv_ref, out_ref, i * CB)
        cols = pl.ds(i * CB, CB)
        pltpu.make_async_copy(out_ref.at[:, :, cols], out_hbm.at[:, :, cols], sem).start()
    pltpu.make_async_copy(out_ref, out_hbm, sem).wait()


def params(mib):
    return pltpu.CompilerParams(vmem_limit_bytes=mib << 20)


def exchange(x, order):
    return lax.all_to_all(
        x, "ctx", split_axis=0, concat_axis=0, axis_index_groups=[order], tiled=True
    )


def per_device(branches, short_taps, long_filter, grad_out):
    lhs1, lhs2, fwd, inv, twist = (jnp.asarray(t) for t in tables())
    tokens, channels = grad_out.shape
    half = GROUP * HALF
    hbm = pl.BlockSpec(memory_space=pltpu.HBM)
    vmem = pl.BlockSpec(memory_space=pltpu.VMEM)
    dma = pltpu.SemaphoreType.DMA
    wire = (BLOCKS, ROWS, CHUNK)
    spectral = (32 // GROUP, half, 2 * CHUNK)
    held = lambda x: pltpu.with_memory_space_constraint(x, pltpu.HBM)
    branches, short_taps, grad_out = map(held, (branches, short_taps, grad_out))
    send = pl.pallas_call(
        head_kernel,
        in_specs=[hbm, hbm, hbm],
        out_specs=hbm,
        out_shape=pltpu.HBM(wire, BF16),
        scratch_shapes=[
            pltpu.VMEM((3, 3, channels), F32),
            pltpu.VMEM((4, tokens, channels), BF16),
            pltpu.VMEM((2, 8, channels), F32),
            pltpu.VMEM(wire, BF16),
            dma,
            dma((3,)),
            dma,
        ],
        compiler_params=params(24),
        name="head",
    )(short_taps, branches, grad_out)
    spectrum = pl.pallas_call(
        filter_kernel,
        in_specs=[vmem] * 4,
        out_specs=vmem,
        out_shape=pltpu.VMEM(spectral, BF16),
        compiler_params=params(32),
        name="filter_spectrum",
    )(long_filter, lhs1, fwd, twist)
    recv = exchange(send, ORDER_IN)
    back, corr = pl.pallas_call(
        middle_kernel,
        in_specs=[vmem] * 7,
        out_specs=[hbm, vmem],
        out_shape=[pltpu.HBM(wire, BF16), pltpu.VMEM(spectral, BF16)],
        scratch_shapes=[pltpu.VMEM(wire, BF16), dma],
        compiler_params=params(32),
        name="middle",
    )(recv, spectrum, lhs1, lhs2, fwd, inv, twist)
    grad_filter, taps, rows = pl.pallas_call(
        grad_filter_kernel,
        in_specs=[hbm, hbm, hbm, vmem, vmem, vmem, vmem],
        out_specs=[vmem, vmem, vmem],
        out_shape=[
            jax.ShapeDtypeStruct(long_filter.shape, F32),
            pltpu.VMEM((3, 3, channels), F32),
            pltpu.VMEM((3, tokens, channels), BF16),
        ],
        scratch_shapes=[
            pltpu.VMEM((2, tokens, channels), BF16),
            dma((3,)),
        ],
        compiler_params=params(32),
        name="grad_filter",
    )(short_taps, branches, grad_out, corr, lhs2, inv, twist)
    returned = exchange(back, ORDER_OUT)
    grads = pl.pallas_call(
        tail_kernel,
        in_specs=[vmem, vmem, vmem],
        out_specs=hbm,
        out_shape=pltpu.HBM(branches.shape, BF16),
        scratch_shapes=[pltpu.VMEM(branches.shape, BF16), dma],
        compiler_params=params(24),
        name="tail",
    )(taps, rows, returned)
    return grads, grad_filter


def solution(mesh):
    in_specs = (P(None, "ctx", "tp"), P(), P(("tp", "ctx"), None), P("ctx", "tp"))
    out_specs = (P(None, "ctx", "tp"), P(("tp", "ctx"), None))
    return jax.shard_map(
        per_device, mesh=mesh, in_specs=in_specs, out_specs=out_specs, check_vma=False
    )
```

```python
import functools

import jax
import jax.numpy as jnp
import ml_dtypes
import numpy as np
from jax import lax
from jax.experimental import pallas as pl
from jax.experimental.pallas import tpu as pltpu
from jax.sharding import PartitionSpec as P

F32 = jnp.float32
BF16 = jnp.bfloat16
CHUNK = 128
BLOCKS = 32
GROUP = 8
SLOT = 16
HALF = BLOCKS
PERIOD = 2 * BLOCKS * CHUNK
ROWS = 72
CB = 256
KB = 128


def ctx_order():
    lexical = [8 * z + 2 * y + x for y in range(4) for x in range(2) for z in range(4)]
    return [lexical[13 * j % BLOCKS] ^ 21 for j in range(BLOCKS)]


ORDER_IN = ctx_order()
ORDER_OUT = ctx_order()
PLACE_IN = [ORDER_IN.index(i) for i in range(BLOCKS)]
PLACE_OUT = [ORDER_OUT.index(i) for i in range(BLOCKS)]


@functools.lru_cache(maxsize=None)
def tables():
    bf = ml_dtypes.bfloat16
    k = np.arange(HALF)[:, None] + 0.5
    m = np.arange(BLOCKS)[None, :]
    eye = np.eye(GROUP)
    phase = 2 * np.pi * k * m / (2 * BLOCKS)
    first = np.stack([np.cos(phase), -np.sin(phase)])
    lhs1 = np.einsum("qkm,st->sqkmt", first[:, :, ORDER_IN], eye).reshape(2 * GROUP * HALF, BLOCKS * GROUP)
    last = np.stack([np.cos(phase), -np.sin(phase)]) * (2.0 / PERIOD)
    lhs2 = np.einsum("qkm,st->mstqk", last[:, :, ORDER_OUT], eye).reshape(BLOCKS * GROUP, 2 * GROUP * HALF)
    r = np.arange(CHUNK)
    cr = 2 * np.pi * (np.outer(r, r) % CHUNK) / CHUNK
    c, s = np.cos(cr), np.sin(cr)
    fwd = np.block([[c, -s], [s, c]])
    inv = np.block([[c, s], [-s, c]])
    tw = 2 * np.pi * k * r[None, :] / PERIOD
    twist = np.stack([np.cos(tw), -np.sin(tw)]).astype(np.float32)
    return lhs1.astype(bf), lhs2.astype(bf), fwd.astype(bf), inv.astype(bf), twist


def take(x, order):
    return jnp.concatenate([x[i : i + 1] for i in order], axis=0)


def runs(places):
    found = []
    for p in sorted(places):
        if found and sum(found[-1]) == p:
            found[-1] = (found[-1][0], found[-1][1] + 1)
        else:
            found.append((p, 1))
    return found


def dot(a, b):
    return jnp.dot(a, b, preferred_element_type=F32)


def taps_slice(taps_ref, channels):
    return taps_ref.at[:, :, pl.ds(pl.multiple_of(lax.axis_index("tp") * channels, 128), channels)]


def featurize(x, taps):
    s0, s1, s2 = taps
    x1 = pltpu.roll(x, 1, 0)
    x2 = pltpu.roll(x, 2, 0)
    feat = s0 * x[8:] + s1 * x1[8:] + s2 * x2[8:]
    row = lax.broadcasted_iota(jnp.int32, (8, x.shape[1]), 0)
    one, two = s1 * x1[:8], s2 * x2[:8]
    first = s0 * x[:8] + jnp.where(row < 1, 0.0, one) + jnp.where(row < 2, 0.0, two)
    tail = jnp.where(row < 1, one, 0.0) + jnp.where(row < 2, two, 0.0)
    return jnp.concatenate([first, feat], axis=0), tail


def head_feat(taps_ref, rows_ref, b, cols):
    taps = [taps_ref[b, j : j + 1, cols] for j in range(3)]
    return featurize(rows_ref[b, :, cols].astype(F32), taps)


def head_store(send_ref, at, rows, value):
    value = value.astype(BF16).T.reshape(KB // 32, 32, CHUNK)
    for n in range(KB // 32):
        send_ref[PLACE_IN[at // 32 + n], rows, :] = value[n]


def head_products(taps_ref, rows_ref, terms_ref, send_ref, at):
    cols = pl.ds(at, KB)
    key, key_tail = head_feat(taps_ref, rows_ref, 1, cols)
    value, value_tail = head_feat(taps_ref, rows_ref, 2, cols)
    head_store(send_ref, at, slice(0, 32), key * value)
    row8 = lax.broadcasted_iota(jnp.int32, (8, KB), 0)
    for i, (k, v) in enumerate(((key[:8], value[:8]), (key_tail, value_tail))):
        terms_ref[i, :, cols] = jnp.where(row8 < 4, pltpu.roll(k, 2, 0), pltpu.roll(v, 4, 0))


def head_gate_grad(taps_ref, rows_ref, terms_ref, send_ref, at):
    cols = pl.ds(at, KB)
    query, query_tail = head_feat(taps_ref, rows_ref, 0, cols)
    go = rows_ref[3, :, cols].astype(F32)
    head_store(send_ref, at, slice(32, 64), go * query)
    row8 = lax.broadcasted_iota(jnp.int32, (8, KB), 0)
    heads = jnp.where(row8 < 6, terms_ref[0, :, cols], pltpu.roll(go[:8], 6, 0))
    heads = jnp.where(row8 < 2, query[:8], heads)
    ends = jnp.where(row8 < 2, query_tail, terms_ref[1, :, cols])
    quarter = lax.broadcasted_iota(jnp.int32, (8, KB), 1) // 8 % 4
    padded = []
    for q in range(4):
        padded += [jnp.where(quarter == q, heads, 0.0), jnp.where(quarter == q, ends, 0.0)]
    padded.append(jnp.zeros((CHUNK - 64, KB), F32))
    terms = jnp.concatenate(padded, axis=0).T.reshape(KB // 32, 4, 8, CHUNK)
    terms = (terms[:, 0] + terms[:, 1] + terms[:, 2] + terms[:, 3]).astype(BF16)
    for n in range(KB // 32):
        send_ref[PLACE_IN[at // 32 + n], 64:72, :] = terms[n]


def head_kernel(
    taps_hbm,
    br_hbm,
    go_hbm,
    send_hbm,
    taps_ref,
    rows_ref,
    terms_ref,
    send_ref,
    taps_sem,
    in_sem,
    out_sem,
):
    channels = rows_ref.shape[2]
    taps_copy = pltpu.make_async_copy(taps_slice(taps_hbm, channels), taps_ref, taps_sem)
    pair_copy = pltpu.make_async_copy(br_hbm.at[1:3], rows_ref.at[1:3], in_sem.at[0])
    query_copy = pltpu.make_async_copy(br_hbm.at[0], rows_ref.at[0], in_sem.at[1])
    go_copy = pltpu.make_async_copy(go_hbm, rows_ref.at[3], in_sem.at[2])
    for copy in (taps_copy, pair_copy, query_copy, go_copy):
        copy.start()
    taps_copy.wait()
    pair_copy.wait()
    for at in range(0, channels, KB):
        head_products(taps_ref, rows_ref, terms_ref, send_ref, at)
    query_copy.wait()
    go_copy.wait()
    for at in range(0, channels, KB):
        head_gate_grad(taps_ref, rows_ref, terms_ref, send_ref, at)
        for first, length in runs(PLACE_IN[at // 32 : (at + KB) // 32]):
            out = pl.ds(first, length)
            pltpu.make_async_copy(send_ref.at[out], send_hbm.at[out], out_sem).start()
    pltpu.make_async_copy(send_ref, send_hbm, out_sem).wait()


def spread(signals, lhs1_ref, twist_ref):
    c, s = twist_ref[0], twist_ref[1]
    first = dot(lhs1_ref[...], jnp.concatenate(signals, axis=1))
    turned = []
    for ch in range(GROUP):
        at = 2 * HALF * ch
        for i in range(len(signals)):
            lanes = slice(CHUNK * i, CHUNK * (i + 1))
            re, im = first[at : at + HALF, lanes], first[at + HALF : at + 2 * HALF, lanes]
            pair = [(re * c - im * s).astype(BF16), (re * s + im * c).astype(BF16)]
            turned.append(jnp.concatenate(pair, axis=1))
    return jnp.concatenate(turned, axis=0)


def forward(signals, lhs1_ref, twist_ref, fwd_ref, apply):
    count = len(signals)
    spectra = dot(spread(signals, lhs1_ref, twist_ref), fwd_ref[...])
    for n in range(GROUP):
        apply(n, [spectra[HALF * (n * count + i) :][:HALF] for i in range(count)])


def gather(value, count, twist_ref):
    c, s = twist_ref[0], twist_ref[1]
    turned = []
    for n in range(GROUP):
        res, ims = [], []
        for i in range(count):
            part = value[HALF * (n * count + i) :][:HALF]
            re, im = part[:, :CHUNK], part[:, CHUNK:]
            res.append((re * c + im * s).astype(BF16))
            ims.append((im * c - re * s).astype(BF16))
        turned.append(jnp.concatenate(res, axis=1))
        turned.append(jnp.concatenate(ims, axis=1))
    return jnp.concatenate(turned, axis=0)


def backward(spectra, lhs2_ref, twist_ref, inv_ref):
    count = len(spectra[0])
    value = dot(jnp.concatenate([x for ch in spectra for x in ch], axis=0), inv_ref[...])
    both = dot(lhs2_ref[...], gather(value, count, twist_ref))
    return [both[:, CHUNK * i : CHUNK * (i + 1)] for i in range(count)]


def filter_kernel(filter_ref, lhs1_ref, fwd_ref, twist_ref, out_ref):
    scale = (BLOCKS * CHUNK) ** -0.5
    for pair in range(2):
        signals = []
        for g in (2 * pair, 2 * pair + 1):
            rows = filter_ref[GROUP * g : GROUP * (g + 1), :] * scale
            stacked = [rows[:, CHUNK * m : CHUNK * (m + 1)] for m in ORDER_IN]
            signals.append(jnp.concatenate(stacked, axis=0).astype(BF16))

        def store(ch, parts):
            rows = slice(HALF * ch, HALF * (ch + 1))
            for i in range(2):
                out_ref[2 * pair + i, rows] = parts[i].astype(BF16)

        forward(signals, lhs1_ref, twist_ref, fwd_ref, store)


def middle_kernel(
    recv_ref,
    spec_ref,
    lhs1_ref,
    lhs2_ref,
    fwd_ref,
    inv_ref,
    twist_ref,
    send_hbm,
    corr_ref,
    send_ref,
    sems,
):
    shape = (BLOCKS, GROUP, CHUNK)
    flat = (BLOCKS * GROUP, CHUNK)
    lane = lax.broadcasted_iota(jnp.int32, (GROUP, CHUNK), 1)
    turn = lambda x, by: pltpu.roll(x, by % CHUNK, 2)
    halo = take(recv_ref[:, 64:72, :].astype(F32), PLACE_IN)
    before = jnp.concatenate([jnp.zeros((1, 8, CHUNK), F32), halo[:-1]], axis=0)
    feat = halo + turn(before, -8)
    prod = take(turn(feat, -2) * turn(feat, -4), ORDER_IN)
    gate = take(feat * turn(halo, -6), ORDER_IN)
    outs, mixes, spreads = [], [], []
    join = lambda re, im: jnp.concatenate([re.astype(BF16), im.astype(BF16)], axis=1)
    for j in range(2):
        both = [recv_ref[:, at + 16 * j : at + 16 * (j + 1), :].astype(F32) for at in (0, 32)]
        for h in range(2):
            g = 2 * j + h
            rows = slice(GROUP * h, GROUP * (h + 1))
            signals = []
            for x, fix in zip(both, (prod, gate)):
                fixed = jnp.where(lane < 2, turn(fix, -SLOT * g), x[:, rows])
                signals.append(fixed.reshape(flat).astype(BF16))
            spreads.append(spread(signals, lhs1_ref, twist_ref))
    size = 2 * GROUP * HALF
    everything = dot(jnp.concatenate(spreads, axis=0), fwd_ref[...])
    for g in range(4):
        spectra = everything[size * g : size * (g + 1)]
        mixed = []
        for ch in range(GROUP):
            at = 2 * HALF * ch
            parts = (spectra[at : at + HALF], spectra[at + HALF : at + 2 * HALF])
            (pr, pi), (gr, gi) = [(x[:, :CHUNK], x[:, CHUNK:]) for x in parts]
            rows = slice(HALF * ch, HALF * (ch + 1))
            hr = spec_ref[g, rows, :CHUNK].astype(F32)
            hi = spec_ref[g, rows, CHUNK:].astype(F32)
            corr_ref[g, rows] = join(pr * gr + pi * gi, pr * gi - pi * gr)
            mixed.append(join(hr * pr - hi * pi, hr * pi + hi * pr))
            mixed.append(join(hr * gr + hi * gi, hr * gi - hi * gr))
        mixes.append(jnp.concatenate(mixed, axis=0))
    everything = dot(jnp.concatenate(mixes, axis=0), inv_ref[...])
    gathers = [gather(everything[size * g : size * (g + 1)], 2, twist_ref) for g in range(4)]
    for j in range(2):
        convs, dzetas = [], []
        for h in range(2):
            value = dot(lhs2_ref[...], gathers[2 * j + h])
            convs.append(value[:, :CHUNK].reshape(shape))
            dzetas.append(value[:, CHUNK:].reshape(shape))
        outs.append((convs, dzetas))
        for i in range(2):
            rows = slice(32 * i + 16 * j, 32 * i + 16 * (j + 1))
            send_ref[:, rows, :] = jnp.concatenate(outs[j][i], axis=1).astype(BF16)
            rows = pl.ds(32 * i + 16 * j, 16)
            pltpu.make_async_copy(send_ref.at[:, rows], send_hbm.at[:, rows], sems.at[0]).start()
    merged = []
    for i in range(2):
        merged.append(outs[0][i][0])
        for g in range(1, 4):
            value = turn(outs[g // 2][i][g % 2], SLOT * g)
            merged[i] = jnp.where(lane < SLOT * g, merged[i], value)
    conv, dzeta = [take(x, PLACE_OUT) for x in merged]
    place = lane % SLOT
    heads = jnp.where(
        place < 2,
        conv * turn(halo, -6),
        jnp.where(place < 4, turn(dzeta, 2) * turn(feat, -2), turn(dzeta, 4) * turn(feat, 2)),
    )
    after = jnp.concatenate([heads[1:], jnp.zeros((1, 8, CHUNK), F32)], axis=0)
    terms = take(jnp.where(place < 8, feat, turn(after, 8)), ORDER_OUT)
    send_ref[:, 64:72, :] = terms.astype(BF16)
    rows = pl.ds(64, 8)
    last = pltpu.make_async_copy(send_ref.at[:, rows], send_hbm.at[:, rows], sems.at[1])
    last.start()
    rows = pl.ds(0, 64)
    pltpu.make_async_copy(send_ref.at[:, rows], send_hbm.at[:, rows], sems.at[0]).wait()
    last.wait()


def grad_filter_kernel(
    taps_hbm,
    br_hbm,
    go_hbm,
    corr_ref,
    lhs2_ref,
    inv_ref,
    twist_ref,
    out_ref,
    taps_ref,
    rows_ref,
    br_ref,
    sems,
):
    channels = go_hbm.shape[1]
    copies = [
        pltpu.make_async_copy(taps_slice(taps_hbm, channels), taps_ref, sems.at[0]),
        pltpu.make_async_copy(br_hbm.at[1:3], br_ref, sems.at[1]),
        pltpu.make_async_copy(go_hbm, rows_ref.at[2], sems.at[2]),
    ]
    for copy in copies:
        copy.start()
    for copy in copies:
        copy.wait()
    for i in range(channels // CB):
        cols = pl.ds(i * CB, CB)
        for b in range(2):
            taps = [taps_ref[b + 1, j : j + 1, cols] for j in range(3)]
            rows_ref[b, :, cols] = featurize(br_ref[b, :, cols].astype(F32), taps)[0].astype(BF16)
    scale = (BLOCKS * CHUNK) ** -0.5
    for pair in range(2):
        spectra = [
            [corr_ref[2 * pair + i, HALF * ch : HALF * (ch + 1)] for i in range(2)]
            for ch in range(GROUP)
        ]
        values = backward(spectra, lhs2_ref, twist_ref, inv_ref)
        for i in range(2):
            at = GROUP * (2 * pair + i)
            for n, m in enumerate(ORDER_OUT):
                out_ref[at : at + GROUP, CHUNK * m : CHUNK * (m + 1)] = (
                    values[i][GROUP * n : GROUP * (n + 1)] * scale
                )


def tail_block(taps_ref, rows_ref, recv_ref, out_ref, at):
    cols = pl.ds(at, CB)
    row8 = lax.broadcasted_iota(jnp.int32, (8, CB), 0)
    places = PLACE_OUT[at // 32 : (at + CB) // 32]
    received = lambda rows: jnp.stack([recv_ref[p, rows, :] for p in places])
    conv = received(slice(0, 32)).reshape(CB, CHUNK).T.astype(F32)
    dzeta = received(slice(32, 64)).reshape(CB, CHUNK).T.astype(F32)
    halo = received(slice(64, 72)).astype(F32)
    turned = [halo] + [pltpu.roll(halo, CHUNK - SLOT * q, 2) for q in range(1, 4)]
    halo = jnp.concatenate(turned, axis=1).reshape(CB, CHUNK).T
    heads, nexts = halo[:8], halo[8:16]

    def with_head(b, at):
        value = rows_ref[b, :, cols].astype(F32)
        first = jnp.where(row8 < 2, pltpu.roll(heads, 8 - at, 0), value[:8])
        return jnp.concatenate([first, value[8:]], axis=0)

    key = with_head(0, 2)
    value = with_head(1, 4)
    grads = (rows_ref[2, :, cols].astype(F32) * conv, dzeta * value, dzeta * key)
    for b in range(3):
        d = grads[b]
        s0, s1, s2 = (taps_ref[b, j : j + 1, cols] for j in range(3))
        d1 = pltpu.roll(d, CHUNK - 1, 0)
        d2 = pltpu.roll(d, CHUNK - 2, 0)
        e1 = jnp.where(row8 < 7, d1[-8:], pltpu.roll(nexts, (7 - 2 * b) % 8, 0))
        e2 = jnp.where(row8 < 6, d2[-8:], pltpu.roll(nexts, (6 - 2 * b) % 8, 0))
        d1 = jnp.concatenate([d1[:-8], e1], axis=0)
        d2 = jnp.concatenate([d2[:-8], e2], axis=0)
        out_ref[b, :, cols] = (s0 * d + s1 * d1 + s2 * d2).astype(BF16)


def tail_kernel(taps_ref, rows_ref, recv_ref, out_hbm, out_ref, sem):
    for i in range(out_ref.shape[2] // CB):
        tail_block(taps_ref, rows_ref, recv_ref, out_ref, i * CB)
        cols = pl.ds(i * CB, CB)
        pltpu.make_async_copy(out_ref.at[:, :, cols], out_hbm.at[:, :, cols], sem).start()
    pltpu.make_async_copy(out_ref, out_hbm, sem).wait()


def params(mib):
    return pltpu.CompilerParams(vmem_limit_bytes=mib << 20)


def exchange(x, order):
    return lax.all_to_all(
        x, "ctx", split_axis=0, concat_axis=0, axis_index_groups=[order], tiled=True
    )


def per_device(branches, short_taps, long_filter, grad_out):
    lhs1, lhs2, fwd, inv, twist = (jnp.asarray(t) for t in tables())
    tokens, channels = grad_out.shape
    half = GROUP * HALF
    hbm = pl.BlockSpec(memory_space=pltpu.HBM)
    vmem = pl.BlockSpec(memory_space=pltpu.VMEM)
    dma = pltpu.SemaphoreType.DMA
    wire = (BLOCKS, ROWS, CHUNK)
    spectral = (32 // GROUP, half, 2 * CHUNK)
    held = lambda x: pltpu.with_memory_space_constraint(x, pltpu.HBM)
    branches, short_taps, grad_out = map(held, (branches, short_taps, grad_out))
    send = pl.pallas_call(
        head_kernel,
        in_specs=[hbm, hbm, hbm],
        out_specs=hbm,
        out_shape=pltpu.HBM(wire, BF16),
        scratch_shapes=[
            pltpu.VMEM((3, 3, channels), F32),
            pltpu.VMEM((4, tokens, channels), BF16),
            pltpu.VMEM((2, 8, channels), F32),
            pltpu.VMEM(wire, BF16),
            dma,
            dma((3,)),
            dma,
        ],
        compiler_params=params(24),
        name="head",
    )(short_taps, branches, grad_out)
    spectrum = pl.pallas_call(
        filter_kernel,
        in_specs=[vmem] * 4,
        out_specs=vmem,
        out_shape=pltpu.VMEM(spectral, BF16),
        compiler_params=params(32),
        name="filter_spectrum",
    )(long_filter, lhs1, fwd, twist)
    recv = exchange(send, ORDER_IN)
    back, corr = pl.pallas_call(
        middle_kernel,
        in_specs=[vmem] * 7,
        out_specs=[hbm, vmem],
        out_shape=[pltpu.HBM(wire, BF16), pltpu.VMEM(spectral, BF16)],
        scratch_shapes=[pltpu.VMEM(wire, BF16), dma((2,))],
        compiler_params=params(32),
        name="middle",
    )(recv, spectrum, lhs1, lhs2, fwd, inv, twist)
    grad_filter, taps, rows = pl.pallas_call(
        grad_filter_kernel,
        in_specs=[hbm, hbm, hbm, vmem, vmem, vmem, vmem],
        out_specs=[vmem, vmem, vmem],
        out_shape=[
            jax.ShapeDtypeStruct(long_filter.shape, F32),
            pltpu.VMEM((3, 3, channels), F32),
            pltpu.VMEM((3, tokens, channels), BF16),
        ],
        scratch_shapes=[
            pltpu.VMEM((2, tokens, channels), BF16),
            dma((3,)),
        ],
        compiler_params=params(32),
        name="grad_filter",
    )(short_taps, branches, grad_out, corr, lhs2, inv, twist)
    returned = exchange(back, ORDER_OUT)
    grads = pl.pallas_call(
        tail_kernel,
        in_specs=[vmem, vmem, vmem],
        out_specs=hbm,
        out_shape=pltpu.HBM(branches.shape, BF16),
        scratch_shapes=[pltpu.VMEM(branches.shape, BF16), dma],
        compiler_params=params(24),
        name="tail",
    )(taps, rows, returned)
    return grads, grad_filter


def solution(mesh):
    in_specs = (P(None, "ctx", "tp"), P(), P(("tp", "ctx"), None), P("ctx", "tp"))
    out_specs = (P(None, "ctx", "tp"), P(("tp", "ctx"), None))
    return jax.shard_map(
        per_device, mesh=mesh, in_specs=in_specs, out_specs=out_specs, check_vma=False
    )
```

```python
import functools

import jax
import jax.numpy as jnp
import ml_dtypes
import numpy as np
from jax import lax
from jax.experimental import pallas as pl
from jax.experimental.pallas import tpu as pltpu
from jax.sharding import PartitionSpec as P

F32 = jnp.float32
BF16 = jnp.bfloat16
CHUNK = 128
BLOCKS = 32
GROUP = 8
SLOT = 16
HALF = BLOCKS
PERIOD = 2 * BLOCKS * CHUNK
ROWS = 72
CB = 256
TAIL_PARTS = (3, 2, 2, 1)
KB = 128


def ctx_order(turn):
    lexical = [8 * z + 2 * (turn * y % 4) + x for y in range(4) for x in range(2) for z in range(4)]
    return [lexical[13 * j % BLOCKS] ^ 21 for j in range(BLOCKS)]


ORDER_IN = ctx_order(1)
ORDER_OUT = ctx_order(-1)
PLACE_IN = [ORDER_IN.index(i) for i in range(BLOCKS)]
PLACE_OUT = [ORDER_OUT.index(i) for i in range(BLOCKS)]


@functools.lru_cache(maxsize=None)
def tables():
    bf = ml_dtypes.bfloat16
    k = np.arange(HALF)[:, None] + 0.5
    m = np.arange(BLOCKS)[None, :]
    eye = np.eye(GROUP)
    phase = 2 * np.pi * k * m / (2 * BLOCKS)
    first = np.stack([np.cos(phase), -np.sin(phase)])
    lhs1 = np.einsum("qkm,st->sqkmt", first[:, :, ORDER_IN], eye).reshape(2 * GROUP * HALF, BLOCKS * GROUP)
    last = np.stack([np.cos(phase), -np.sin(phase)]) * (2.0 / PERIOD)
    lhs2 = np.einsum("qkm,st->mstqk", last[:, :, ORDER_OUT], eye).reshape(BLOCKS * GROUP, 2 * GROUP * HALF)
    r = np.arange(CHUNK)
    cr = 2 * np.pi * (np.outer(r, r) % CHUNK) / CHUNK
    c, s = np.cos(cr), np.sin(cr)
    fwd = np.block([[c, -s], [s, c]])
    inv = np.block([[c, s], [-s, c]])
    tw = 2 * np.pi * k * r[None, :] / PERIOD
    twist = np.stack([np.cos(tw), -np.sin(tw)]).astype(np.float32)
    return lhs1.astype(bf), lhs2.astype(bf), fwd.astype(bf), inv.astype(bf), twist


def take(x, order):
    return jnp.concatenate([x[i : i + 1] for i in order], axis=0)


def runs(places):
    found = []
    for p in sorted(places):
        if found and sum(found[-1]) == p:
            found[-1] = (found[-1][0], found[-1][1] + 1)
        else:
            found.append((p, 1))
    return found


def dot(a, b):
    return jnp.dot(a, b, preferred_element_type=F32)


def taps_slice(taps_ref, channels):
    return taps_ref.at[:, :, pl.ds(pl.multiple_of(lax.axis_index("tp") * channels, 128), channels)]


def featurize(x, taps):
    s0, s1, s2 = taps
    x1 = pltpu.roll(x, 1, 0)
    x2 = pltpu.roll(x, 2, 0)
    feat = s0 * x[8:] + s1 * x1[8:] + s2 * x2[8:]
    row = lax.broadcasted_iota(jnp.int32, (8, x.shape[1]), 0)
    one, two = s1 * x1[:8], s2 * x2[:8]
    first = s0 * x[:8] + jnp.where(row < 1, 0.0, one) + jnp.where(row < 2, 0.0, two)
    tail = jnp.where(row < 1, one, 0.0) + jnp.where(row < 2, two, 0.0)
    return jnp.concatenate([first, feat], axis=0), tail


def head_feat(taps_ref, rows_ref, b, cols):
    taps = [taps_ref[b, j : j + 1, cols] for j in range(3)]
    return featurize(rows_ref[b, :, cols].astype(F32), taps)


def head_store(send_ref, at, rows, value):
    value = value.astype(BF16).T.reshape(KB // 32, 32, CHUNK)
    for n in range(KB // 32):
        send_ref[PLACE_IN[at // 32 + n], rows, :] = value[n]


def head_products(taps_ref, rows_ref, terms_ref, send_ref, at):
    cols = pl.ds(at, KB)
    key, key_tail = head_feat(taps_ref, rows_ref, 1, cols)
    value, value_tail = head_feat(taps_ref, rows_ref, 2, cols)
    head_store(send_ref, at, slice(0, 32), key * value)
    row8 = lax.broadcasted_iota(jnp.int32, (8, KB), 0)
    for i, (k, v) in enumerate(((key[:8], value[:8]), (key_tail, value_tail))):
        terms_ref[i, :, cols] = jnp.where(row8 < 4, pltpu.roll(k, 2, 0), pltpu.roll(v, 4, 0))


def head_gate_grad(taps_ref, rows_ref, terms_ref, send_ref, at):
    cols = pl.ds(at, KB)
    query, query_tail = head_feat(taps_ref, rows_ref, 0, cols)
    go = rows_ref[3, :, cols].astype(F32)
    head_store(send_ref, at, slice(32, 64), go * query)
    row8 = lax.broadcasted_iota(jnp.int32, (8, KB), 0)
    heads = jnp.where(row8 < 6, terms_ref[0, :, cols], pltpu.roll(go[:8], 6, 0))
    heads = jnp.where(row8 < 2, query[:8], heads)
    ends = jnp.where(row8 < 2, query_tail, terms_ref[1, :, cols])
    quarter = lax.broadcasted_iota(jnp.int32, (8, KB), 1) // 8 % 4
    padded = []
    for q in range(4):
        padded += [jnp.where(quarter == q, heads, 0.0), jnp.where(quarter == q, ends, 0.0)]
    padded.append(jnp.zeros((CHUNK - 64, KB), F32))
    terms = jnp.concatenate(padded, axis=0).T.reshape(KB // 32, 4, 8, CHUNK)
    terms = (terms[:, 0] + terms[:, 1] + terms[:, 2] + terms[:, 3]).astype(BF16)
    for n in range(KB // 32):
        send_ref[PLACE_IN[at // 32 + n], 64:72, :] = terms[n]


def head_kernel(
    taps_hbm,
    br_hbm,
    go_hbm,
    send_hbm,
    taps_ref,
    rows_ref,
    terms_ref,
    send_ref,
    taps_sem,
    in_sem,
    out_sem,
):
    channels = rows_ref.shape[2]
    taps_copy = pltpu.make_async_copy(taps_slice(taps_hbm, channels), taps_ref, taps_sem)
    pair_copy = pltpu.make_async_copy(br_hbm.at[1:3], rows_ref.at[1:3], in_sem.at[0])
    query_copy = pltpu.make_async_copy(br_hbm.at[0], rows_ref.at[0], in_sem.at[1])
    go_copy = pltpu.make_async_copy(go_hbm, rows_ref.at[3], in_sem.at[2])
    for copy in (taps_copy, pair_copy, query_copy, go_copy):
        copy.start()
    taps_copy.wait()
    pair_copy.wait()
    for at in range(0, channels, KB):
        head_products(taps_ref, rows_ref, terms_ref, send_ref, at)
    query_copy.wait()
    go_copy.wait()
    for at in range(0, channels, KB):
        head_gate_grad(taps_ref, rows_ref, terms_ref, send_ref, at)
        for first, length in runs(PLACE_IN[at // 32 : (at + KB) // 32]):
            out = pl.ds(first, length)
            pltpu.make_async_copy(send_ref.at[out], send_hbm.at[out], out_sem).start()
    pltpu.make_async_copy(send_ref, send_hbm, out_sem).wait()


def spread(signals, lhs1_ref, twist_ref):
    c, s = twist_ref[0], twist_ref[1]
    first = dot(lhs1_ref[...], jnp.concatenate(signals, axis=1))
    turned = []
    for ch in range(GROUP):
        at = 2 * HALF * ch
        for i in range(len(signals)):
            lanes = slice(CHUNK * i, CHUNK * (i + 1))
            re, im = first[at : at + HALF, lanes], first[at + HALF : at + 2 * HALF, lanes]
            pair = [(re * c - im * s).astype(BF16), (re * s + im * c).astype(BF16)]
            turned.append(jnp.concatenate(pair, axis=1))
    return jnp.concatenate(turned, axis=0)


def forward(signals, lhs1_ref, twist_ref, fwd_ref, apply):
    count = len(signals)
    spectra = dot(spread(signals, lhs1_ref, twist_ref), fwd_ref[...])
    for n in range(GROUP):
        apply(n, [spectra[HALF * (n * count + i) :][:HALF] for i in range(count)])


def gather(value, count, twist_ref):
    c, s = twist_ref[0], twist_ref[1]
    turned = []
    for n in range(GROUP):
        res, ims = [], []
        for i in range(count):
            part = value[HALF * (n * count + i) :][:HALF]
            re, im = part[:, :CHUNK], part[:, CHUNK:]
            res.append((re * c + im * s).astype(BF16))
            ims.append((im * c - re * s).astype(BF16))
        turned.append(jnp.concatenate(res, axis=1))
        turned.append(jnp.concatenate(ims, axis=1))
    return jnp.concatenate(turned, axis=0)


def backward(spectra, lhs2_ref, twist_ref, inv_ref):
    count = len(spectra[0])
    value = dot(jnp.concatenate([x for ch in spectra for x in ch], axis=0), inv_ref[...])
    both = dot(lhs2_ref[...], gather(value, count, twist_ref))
    return [both[:, CHUNK * i : CHUNK * (i + 1)] for i in range(count)]


def filter_kernel(filter_ref, lhs1_ref, fwd_ref, twist_ref, out_ref):
    scale = (BLOCKS * CHUNK) ** -0.5
    for pair in range(2):
        signals = []
        for g in (2 * pair, 2 * pair + 1):
            rows = filter_ref[GROUP * g : GROUP * (g + 1), :] * scale
            stacked = [rows[:, CHUNK * m : CHUNK * (m + 1)] for m in ORDER_IN]
            signals.append(jnp.concatenate(stacked, axis=0).astype(BF16))

        def store(ch, parts):
            rows = slice(HALF * ch, HALF * (ch + 1))
            for i in range(2):
                out_ref[2 * pair + i, rows] = parts[i].astype(BF16)

        forward(signals, lhs1_ref, twist_ref, fwd_ref, store)


def middle_kernel(
    recv_ref,
    spec_ref,
    lhs1_ref,
    lhs2_ref,
    fwd_ref,
    inv_ref,
    twist_ref,
    send_hbm,
    corr_ref,
    send_ref,
    sems,
):
    shape = (BLOCKS, GROUP, CHUNK)
    flat = (BLOCKS * GROUP, CHUNK)
    lane = lax.broadcasted_iota(jnp.int32, (GROUP, CHUNK), 1)
    turn = lambda x, by: pltpu.roll(x, by % CHUNK, 2)
    halo = take(recv_ref[:, 64:72, :].astype(F32), PLACE_IN)
    before = jnp.concatenate([jnp.zeros((1, 8, CHUNK), F32), halo[:-1]], axis=0)
    feat = halo + turn(before, -8)
    prod = take(turn(feat, -2) * turn(feat, -4), ORDER_IN)
    gate = take(feat * turn(halo, -6), ORDER_IN)
    outs, mixes, spreads = [], [], []
    join = lambda re, im: jnp.concatenate([re.astype(BF16), im.astype(BF16)], axis=1)
    for j in range(2):
        both = [recv_ref[:, at + 16 * j : at + 16 * (j + 1), :].astype(F32) for at in (0, 32)]
        for h in range(2):
            g = 2 * j + h
            rows = slice(GROUP * h, GROUP * (h + 1))
            signals = []
            for x, fix in zip(both, (prod, gate)):
                fixed = jnp.where(lane < 2, turn(fix, -SLOT * g), x[:, rows])
                signals.append(fixed.reshape(flat).astype(BF16))
            spreads.append(spread(signals, lhs1_ref, twist_ref))
    size = 2 * GROUP * HALF
    everything = dot(jnp.concatenate(spreads, axis=0), fwd_ref[...])
    for g in range(4):
        spectra = everything[size * g : size * (g + 1)]
        mixed = []
        for ch in range(GROUP):
            at = 2 * HALF * ch
            parts = (spectra[at : at + HALF], spectra[at + HALF : at + 2 * HALF])
            (pr, pi), (gr, gi) = [(x[:, :CHUNK], x[:, CHUNK:]) for x in parts]
            rows = slice(HALF * ch, HALF * (ch + 1))
            hr = spec_ref[g, rows, :CHUNK].astype(F32)
            hi = spec_ref[g, rows, CHUNK:].astype(F32)
            corr_ref[g, rows] = join(pr * gr + pi * gi, pr * gi - pi * gr)
            mixed.append(join(hr * pr - hi * pi, hr * pi + hi * pr))
            mixed.append(join(hr * gr + hi * gi, hr * gi - hi * gr))
        mixes.append(jnp.concatenate(mixed, axis=0))
    everything = dot(jnp.concatenate(mixes, axis=0), inv_ref[...])
    gathers = [gather(everything[size * g : size * (g + 1)], 2, twist_ref) for g in range(4)]
    for j in range(2):
        convs, dzetas = [], []
        for h in range(2):
            value = dot(lhs2_ref[...], gathers[2 * j + h])
            convs.append(value[:, :CHUNK].reshape(shape))
            dzetas.append(value[:, CHUNK:].reshape(shape))
        outs.append((convs, dzetas))
        for i in range(2):
            rows = slice(32 * j + 16 * i, 32 * j + 16 * (i + 1))
            send_ref[:, rows, :] = jnp.concatenate(outs[j][i], axis=1).astype(BF16)
        rows = pl.ds(32 * j, 32)
        pltpu.make_async_copy(send_ref.at[:, rows], send_hbm.at[:, rows], sems.at[0]).start()
    merged = []
    for i in range(2):
        merged.append(outs[0][i][0])
        for g in range(1, 4):
            value = turn(outs[g // 2][i][g % 2], SLOT * g)
            merged[i] = jnp.where(lane < SLOT * g, merged[i], value)
    conv, dzeta = [take(x, PLACE_OUT) for x in merged]
    place = lane % SLOT
    heads = jnp.where(
        place < 2,
        conv * turn(halo, -6),
        jnp.where(place < 4, turn(dzeta, 2) * turn(feat, -2), turn(dzeta, 4) * turn(feat, 2)),
    )
    after = jnp.concatenate([heads[1:], jnp.zeros((1, 8, CHUNK), F32)], axis=0)
    terms = take(jnp.where(place < 8, feat, turn(after, 8)), ORDER_OUT)
    send_ref[:, 64:72, :] = terms.astype(BF16)
    rows = pl.ds(64, 8)
    last = pltpu.make_async_copy(send_ref.at[:, rows], send_hbm.at[:, rows], sems.at[1])
    last.start()
    rows = pl.ds(0, 64)
    pltpu.make_async_copy(send_ref.at[:, rows], send_hbm.at[:, rows], sems.at[0]).wait()
    last.wait()


def grad_filter_kernel(
    taps_hbm,
    br_hbm,
    go_hbm,
    corr_ref,
    lhs2_ref,
    inv_ref,
    twist_ref,
    out_ref,
    taps_ref,
    rows_ref,
    br_ref,
    sems,
):
    channels = go_hbm.shape[1]
    copies = [
        pltpu.make_async_copy(taps_slice(taps_hbm, channels), taps_ref, sems.at[0]),
        pltpu.make_async_copy(br_hbm.at[1:3], br_ref, sems.at[1]),
        pltpu.make_async_copy(go_hbm, rows_ref.at[2], sems.at[2]),
    ]
    for copy in copies:
        copy.start()
    for copy in copies:
        copy.wait()
    for i in range(channels // CB):
        cols = pl.ds(i * CB, CB)
        for b in range(2):
            taps = [taps_ref[b + 1, j : j + 1, cols] for j in range(3)]
            rows_ref[b, :, cols] = featurize(br_ref[b, :, cols].astype(F32), taps)[0].astype(BF16)
    scale = (BLOCKS * CHUNK) ** -0.5
    for pair in range(2):
        spectra = [
            [corr_ref[2 * pair + i, HALF * ch : HALF * (ch + 1)] for i in range(2)]
            for ch in range(GROUP)
        ]
        values = backward(spectra, lhs2_ref, twist_ref, inv_ref)
        for i in range(2):
            at = GROUP * (2 * pair + i)
            for n, m in enumerate(ORDER_OUT):
                out_ref[at : at + GROUP, CHUNK * m : CHUNK * (m + 1)] = (
                    values[i][GROUP * n : GROUP * (n + 1)] * scale
                )


def tail_block(taps_ref, rows_ref, recv_ref, out_ref, at, size):
    cols = pl.ds(at, size)
    row8 = lax.broadcasted_iota(jnp.int32, (8, size), 0)
    places = PLACE_OUT[at // 32 : (at + size) // 32]
    conv = [recv_ref[p, i : i + 16, :] for p in places for i in (0, 32)]
    dzeta = [recv_ref[p, i : i + 16, :] for p in places for i in (16, 48)]
    conv = jnp.concatenate(conv, axis=0).T.astype(F32)
    dzeta = jnp.concatenate(dzeta, axis=0).T.astype(F32)
    halo = jnp.stack([recv_ref[p, 64:72, :] for p in places]).astype(F32)
    turned = [halo] + [pltpu.roll(halo, CHUNK - SLOT * q, 2) for q in range(1, 4)]
    halo = jnp.concatenate(turned, axis=1).reshape(size, CHUNK).T
    heads, nexts = halo[:8], halo[8:16]

    def with_head(b, at):
        value = rows_ref[b, :, cols].astype(F32)
        first = jnp.where(row8 < 2, pltpu.roll(heads, 8 - at, 0), value[:8])
        return jnp.concatenate([first, value[8:]], axis=0)

    key = with_head(0, 2)
    value = with_head(1, 4)
    grads = (rows_ref[2, :, cols].astype(F32) * conv, dzeta * value, dzeta * key)
    for b in range(3):
        d = grads[b]
        s0, s1, s2 = (taps_ref[b, j : j + 1, cols] for j in range(3))
        d1 = pltpu.roll(d, CHUNK - 1, 0)
        d2 = pltpu.roll(d, CHUNK - 2, 0)
        e1 = jnp.where(row8 < 7, d1[-8:], pltpu.roll(nexts, (7 - 2 * b) % 8, 0))
        e2 = jnp.where(row8 < 6, d2[-8:], pltpu.roll(nexts, (6 - 2 * b) % 8, 0))
        d1 = jnp.concatenate([d1[:-8], e1], axis=0)
        d2 = jnp.concatenate([d2[:-8], e2], axis=0)
        out_ref[b, :, cols] = (s0 * d + s1 * d1 + s2 * d2).astype(BF16)


def tail_kernel(taps_ref, rows_ref, recv_ref, out_hbm, out_ref, sem):
    at = 0
    for part in TAIL_PARTS:
        size = out_ref.shape[2] * part // 8
        tail_block(taps_ref, rows_ref, recv_ref, out_ref, at, size)
        cols = pl.ds(at, size)
        pltpu.make_async_copy(out_ref.at[:, :, cols], out_hbm.at[:, :, cols], sem).start()
        at += size
    pltpu.make_async_copy(out_ref, out_hbm, sem).wait()


def params(mib):
    return pltpu.CompilerParams(vmem_limit_bytes=mib << 20)


def exchange(x, order):
    return lax.all_to_all(
        x, "ctx", split_axis=0, concat_axis=0, axis_index_groups=[order], tiled=True
    )


def per_device(branches, short_taps, long_filter, grad_out):
    lhs1, lhs2, fwd, inv, twist = (jnp.asarray(t) for t in tables())
    tokens, channels = grad_out.shape
    half = GROUP * HALF
    hbm = pl.BlockSpec(memory_space=pltpu.HBM)
    vmem = pl.BlockSpec(memory_space=pltpu.VMEM)
    dma = pltpu.SemaphoreType.DMA
    wire = (BLOCKS, ROWS, CHUNK)
    spectral = (32 // GROUP, half, 2 * CHUNK)
    held = lambda x: pltpu.with_memory_space_constraint(x, pltpu.HBM)
    branches, short_taps, grad_out = map(held, (branches, short_taps, grad_out))
    send = pl.pallas_call(
        head_kernel,
        in_specs=[hbm, hbm, hbm],
        out_specs=hbm,
        out_shape=pltpu.HBM(wire, BF16),
        scratch_shapes=[
            pltpu.VMEM((3, 3, channels), F32),
            pltpu.VMEM((4, tokens, channels), BF16),
            pltpu.VMEM((2, 8, channels), F32),
            pltpu.VMEM(wire, BF16),
            dma,
            dma((3,)),
            dma,
        ],
        compiler_params=params(24),
        name="head",
    )(short_taps, branches, grad_out)
    spectrum = pl.pallas_call(
        filter_kernel,
        in_specs=[vmem] * 4,
        out_specs=vmem,
        out_shape=pltpu.VMEM(spectral, BF16),
        compiler_params=params(32),
        name="filter_spectrum",
    )(long_filter, lhs1, fwd, twist)
    recv = exchange(send, ORDER_IN)
    back, corr = pl.pallas_call(
        middle_kernel,
        in_specs=[vmem] * 7,
        out_specs=[hbm, vmem],
        out_shape=[pltpu.HBM(wire, BF16), pltpu.VMEM(spectral, BF16)],
        scratch_shapes=[pltpu.VMEM(wire, BF16), dma((2,))],
        compiler_params=params(32),
        name="middle",
    )(recv, spectrum, lhs1, lhs2, fwd, inv, twist)
    grad_filter, taps, rows = pl.pallas_call(
        grad_filter_kernel,
        in_specs=[hbm, hbm, hbm, vmem, vmem, vmem, vmem],
        out_specs=[vmem, vmem, vmem],
        out_shape=[
            jax.ShapeDtypeStruct(long_filter.shape, F32),
            pltpu.VMEM((3, 3, channels), F32),
            pltpu.VMEM((3, tokens, channels), BF16),
        ],
        scratch_shapes=[
            pltpu.VMEM((2, tokens, channels), BF16),
            dma((3,)),
        ],
        compiler_params=params(32),
        name="grad_filter",
    )(short_taps, branches, grad_out, corr, lhs2, inv, twist)
    returned = exchange(back, ORDER_OUT)
    grads = pl.pallas_call(
        tail_kernel,
        in_specs=[vmem, vmem, vmem],
        out_specs=hbm,
        out_shape=pltpu.HBM(branches.shape, BF16),
        scratch_shapes=[pltpu.VMEM(branches.shape, BF16), dma],
        compiler_params=params(24),
        name="tail",
    )(taps, rows, returned)
    return grads, grad_filter


def solution(mesh):
    in_specs = (P(None, "ctx", "tp"), P(), P(("tp", "ctx"), None), P("ctx", "tp"))
    out_specs = (P(None, "ctx", "tp"), P(("tp", "ctx"), None))
    return jax.shard_map(
        per_device, mesh=mesh, in_specs=in_specs, out_specs=out_specs, check_vma=False
    )
```

```python
import functools

import jax
import jax.numpy as jnp
import ml_dtypes
import numpy as np
from jax import lax
from jax.experimental import pallas as pl
from jax.experimental.pallas import tpu as pltpu
from jax.sharding import PartitionSpec as P

F32 = jnp.float32
BF16 = jnp.bfloat16
CHUNK = 128
BLOCKS = 32
GROUP = 8
SLOT = 16
HALF = BLOCKS
PERIOD = 2 * BLOCKS * CHUNK
ROWS = 72
CB = 256
TAIL_PARTS = (3, 2, 2, 1)
KB = 128


def ctx_order(turn):
    lexical = [8 * z + 2 * (turn * y % 4) + x for y in range(4) for x in range(2) for z in range(4)]
    return [lexical[13 * j % BLOCKS] ^ 21 for j in range(BLOCKS)]


ORDER_IN = ctx_order(1)
ORDER_OUT = ctx_order(-1)
PLACE_IN = [ORDER_IN.index(i) for i in range(BLOCKS)]
PLACE_OUT = [ORDER_OUT.index(i) for i in range(BLOCKS)]


@functools.lru_cache(maxsize=None)
def tables():
    bf = ml_dtypes.bfloat16
    k = np.arange(HALF)[:, None] + 0.5
    m = np.arange(BLOCKS)[None, :]
    eye = np.eye(GROUP)
    phase = 2 * np.pi * k * m / (2 * BLOCKS)
    first = np.stack([np.cos(phase), -np.sin(phase)])
    lhs1 = np.einsum("qkm,st->sqkmt", first[:, :, ORDER_IN], eye).reshape(2 * GROUP * HALF, BLOCKS * GROUP)
    last = np.stack([np.cos(phase), -np.sin(phase)]) * (2.0 / PERIOD)
    lhs2 = np.einsum("qkm,st->mstqk", last[:, :, ORDER_OUT], eye).reshape(BLOCKS * GROUP, 2 * GROUP * HALF)
    r = np.arange(CHUNK)
    cr = 2 * np.pi * (np.outer(r, r) % CHUNK) / CHUNK
    c, s = np.cos(cr), np.sin(cr)
    fwd = np.block([[c, -s], [s, c]])
    inv = np.block([[c, s], [-s, c]])
    tw = 2 * np.pi * k * r[None, :] / PERIOD
    twist = np.stack([np.cos(tw), -np.sin(tw)]).astype(np.float32)
    return lhs1.astype(bf), lhs2.astype(bf), fwd.astype(bf), inv.astype(bf), twist


def take(x, order):
    return jnp.concatenate([x[i : i + 1] for i in order], axis=0)


def runs(places):
    found = []
    for p in sorted(places):
        if found and sum(found[-1]) == p:
            found[-1] = (found[-1][0], found[-1][1] + 1)
        else:
            found.append((p, 1))
    return found


def dot(a, b):
    return jnp.dot(a, b, preferred_element_type=F32)


def taps_slice(taps_ref, channels):
    return taps_ref.at[:, :, pl.ds(pl.multiple_of(lax.axis_index("tp") * channels, 128), channels)]


def featurize(x, taps):
    s0, s1, s2 = taps
    x1 = pltpu.roll(x, 1, 0)
    x2 = pltpu.roll(x, 2, 0)
    feat = s0 * x[8:] + s1 * x1[8:] + s2 * x2[8:]
    row = lax.broadcasted_iota(jnp.int32, (8, x.shape[1]), 0)
    one, two = s1 * x1[:8], s2 * x2[:8]
    first = s0 * x[:8] + jnp.where(row < 1, 0.0, one) + jnp.where(row < 2, 0.0, two)
    tail = jnp.where(row < 1, one, 0.0) + jnp.where(row < 2, two, 0.0)
    return jnp.concatenate([first, feat], axis=0), tail


def head_feat(taps_ref, rows_ref, b, cols):
    taps = [taps_ref[b, j : j + 1, cols] for j in range(3)]
    return featurize(rows_ref[b, :, cols].astype(F32), taps)


def head_store(send_ref, at, rows, value):
    value = value.astype(BF16).T.reshape(KB // 32, 32, CHUNK)
    for n in range(KB // 32):
        send_ref[PLACE_IN[at // 32 + n], rows, :] = value[n]


def head_products(taps_ref, rows_ref, terms_ref, send_ref, at):
    cols = pl.ds(at, KB)
    key, key_tail = head_feat(taps_ref, rows_ref, 1, cols)
    value, value_tail = head_feat(taps_ref, rows_ref, 2, cols)
    head_store(send_ref, at, slice(0, 32), key * value)
    row8 = lax.broadcasted_iota(jnp.int32, (8, KB), 0)
    for i, (k, v) in enumerate(((key[:8], value[:8]), (key_tail, value_tail))):
        terms_ref[i, :, cols] = jnp.where(row8 < 4, pltpu.roll(k, 2, 0), pltpu.roll(v, 4, 0))


def head_gate_grad(taps_ref, rows_ref, terms_ref, send_ref, at):
    cols = pl.ds(at, KB)
    query, query_tail = head_feat(taps_ref, rows_ref, 0, cols)
    go = rows_ref[3, :, cols].astype(F32)
    head_store(send_ref, at, slice(32, 64), go * query)
    row8 = lax.broadcasted_iota(jnp.int32, (8, KB), 0)
    heads = jnp.where(row8 < 6, terms_ref[0, :, cols], pltpu.roll(go[:8], 6, 0))
    heads = jnp.where(row8 < 2, query[:8], heads)
    ends = jnp.where(row8 < 2, query_tail, terms_ref[1, :, cols])
    quarter = lax.broadcasted_iota(jnp.int32, (8, KB), 1) // 8 % 4
    padded = []
    for q in range(4):
        padded += [jnp.where(quarter == q, heads, 0.0), jnp.where(quarter == q, ends, 0.0)]
    padded.append(jnp.zeros((CHUNK - 64, KB), F32))
    terms = jnp.concatenate(padded, axis=0).T.reshape(KB // 32, 4, 8, CHUNK)
    terms = (terms[:, 0] + terms[:, 1] + terms[:, 2] + terms[:, 3]).astype(BF16)
    for n in range(KB // 32):
        send_ref[PLACE_IN[at // 32 + n], 64:72, :] = terms[n]


def head_kernel(
    taps_hbm,
    br_hbm,
    go_hbm,
    send_hbm,
    taps_ref,
    rows_ref,
    terms_ref,
    send_ref,
    taps_sem,
    in_sem,
    out_sem,
):
    channels = rows_ref.shape[2]
    taps_copy = pltpu.make_async_copy(taps_slice(taps_hbm, channels), taps_ref, taps_sem)
    pair_copy = pltpu.make_async_copy(br_hbm.at[1:3], rows_ref.at[1:3], in_sem.at[0])
    query_copy = pltpu.make_async_copy(br_hbm.at[0], rows_ref.at[0], in_sem.at[1])
    go_copy = pltpu.make_async_copy(go_hbm, rows_ref.at[3], in_sem.at[2])
    for copy in (taps_copy, pair_copy, query_copy, go_copy):
        copy.start()
    taps_copy.wait()
    pair_copy.wait()
    for at in range(0, channels, KB):
        head_products(taps_ref, rows_ref, terms_ref, send_ref, at)
    done = pl.ds(0, 32)
    early = pltpu.make_async_copy(send_ref.at[:, done], send_hbm.at[:, done], in_sem.at[0])
    early.start()
    rest = pl.ds(32, ROWS - 32)
    query_copy.wait()
    go_copy.wait()
    for at in range(0, channels, KB):
        head_gate_grad(taps_ref, rows_ref, terms_ref, send_ref, at)
        for first, length in runs(PLACE_IN[at // 32 : (at + KB) // 32]):
            out = pl.ds(first, length)
            pltpu.make_async_copy(send_ref.at[out, rest], send_hbm.at[out, rest], out_sem).start()
    early.wait()
    pltpu.make_async_copy(send_ref.at[:, rest], send_hbm.at[:, rest], out_sem).wait()


def spread(signals, lhs1_ref, twist_ref):
    c, s = twist_ref[0], twist_ref[1]
    first = dot(lhs1_ref[...], jnp.concatenate(signals, axis=1))
    turned = []
    for ch in range(GROUP):
        at = 2 * HALF * ch
        for i in range(len(signals)):
            lanes = slice(CHUNK * i, CHUNK * (i + 1))
            re, im = first[at : at + HALF, lanes], first[at + HALF : at + 2 * HALF, lanes]
            pair = [(re * c - im * s).astype(BF16), (re * s + im * c).astype(BF16)]
            turned.append(jnp.concatenate(pair, axis=1))
    return jnp.concatenate(turned, axis=0)


def forward(signals, lhs1_ref, twist_ref, fwd_ref, apply):
    count = len(signals)
    spectra = dot(spread(signals, lhs1_ref, twist_ref), fwd_ref[...])
    for n in range(GROUP):
        apply(n, [spectra[HALF * (n * count + i) :][:HALF] for i in range(count)])


def gather(value, count, twist_ref):
    c, s = twist_ref[0], twist_ref[1]
    turned = []
    for n in range(GROUP):
        res, ims = [], []
        for i in range(count):
            part = value[HALF * (n * count + i) :][:HALF]
            re, im = part[:, :CHUNK], part[:, CHUNK:]
            res.append((re * c + im * s).astype(BF16))
            ims.append((im * c - re * s).astype(BF16))
        turned.append(jnp.concatenate(res, axis=1))
        turned.append(jnp.concatenate(ims, axis=1))
    return jnp.concatenate(turned, axis=0)


def backward(spectra, lhs2_ref, twist_ref, inv_ref):
    count = len(spectra[0])
    value = dot(jnp.concatenate([x for ch in spectra for x in ch], axis=0), inv_ref[...])
    both = dot(lhs2_ref[...], gather(value, count, twist_ref))
    return [both[:, CHUNK * i : CHUNK * (i + 1)] for i in range(count)]


def filter_kernel(filter_ref, lhs1_ref, fwd_ref, twist_ref, out_ref):
    scale = (BLOCKS * CHUNK) ** -0.5
    for pair in range(2):
        signals = []
        for g in (2 * pair, 2 * pair + 1):
            rows = filter_ref[GROUP * g : GROUP * (g + 1), :] * scale
            stacked = [rows[:, CHUNK * m : CHUNK * (m + 1)] for m in ORDER_IN]
            signals.append(jnp.concatenate(stacked, axis=0).astype(BF16))

        def store(ch, parts):
            rows = slice(HALF * ch, HALF * (ch + 1))
            for i in range(2):
                out_ref[2 * pair + i, rows] = parts[i].astype(BF16)

        forward(signals, lhs1_ref, twist_ref, fwd_ref, store)


def middle_kernel(
    recv_ref,
    spec_ref,
    lhs1_ref,
    lhs2_ref,
    fwd_ref,
    inv_ref,
    twist_ref,
    send_hbm,
    corr_ref,
    send_ref,
    sems,
):
    shape = (BLOCKS, GROUP, CHUNK)
    flat = (BLOCKS * GROUP, CHUNK)
    lane = lax.broadcasted_iota(jnp.int32, (GROUP, CHUNK), 1)
    turn = lambda x, by: pltpu.roll(x, by % CHUNK, 2)
    halo = take(recv_ref[:, 64:72, :].astype(F32), PLACE_IN)
    before = jnp.concatenate([jnp.zeros((1, 8, CHUNK), F32), halo[:-1]], axis=0)
    feat = halo + turn(before, -8)
    prod = take(turn(feat, -2) * turn(feat, -4), ORDER_IN)
    gate = take(feat * turn(halo, -6), ORDER_IN)
    outs, mixes, spreads = [], [], []
    join = lambda re, im: jnp.concatenate([re.astype(BF16), im.astype(BF16)], axis=1)
    for j in range(2):
        both = [recv_ref[:, at + 16 * j : at + 16 * (j + 1), :].astype(F32) for at in (0, 32)]
        for h in range(2):
            g = 2 * j + h
            rows = slice(GROUP * h, GROUP * (h + 1))
            signals = []
            for x, fix in zip(both, (prod, gate)):
                fixed = jnp.where(lane < 2, turn(fix, -SLOT * g), x[:, rows])
                signals.append(fixed.reshape(flat).astype(BF16))
            spreads.append(spread(signals, lhs1_ref, twist_ref))
    size = 2 * GROUP * HALF
    everything = dot(jnp.concatenate(spreads, axis=0), fwd_ref[...])
    for g in range(4):
        spectra = everything[size * g : size * (g + 1)]
        mixed = []
        for ch in range(GROUP):
            at = 2 * HALF * ch
            parts = (spectra[at : at + HALF], spectra[at + HALF : at + 2 * HALF])
            (pr, pi), (gr, gi) = [(x[:, :CHUNK], x[:, CHUNK:]) for x in parts]
            rows = slice(HALF * ch, HALF * (ch + 1))
            hr = spec_ref[g, rows, :CHUNK].astype(F32)
            hi = spec_ref[g, rows, CHUNK:].astype(F32)
            corr_ref[g, rows] = join(pr * gr + pi * gi, pr * gi - pi * gr)
            mixed.append(join(hr * pr - hi * pi, hr * pi + hi * pr))
            mixed.append(join(hr * gr + hi * gi, hr * gi - hi * gr))
        mixes.append(jnp.concatenate(mixed, axis=0))
    everything = dot(jnp.concatenate(mixes, axis=0), inv_ref[...])
    gathers = [gather(everything[size * g : size * (g + 1)], 2, twist_ref) for g in range(4)]
    for j in range(2):
        convs, dzetas = [], []
        for h in range(2):
            value = dot(lhs2_ref[...], gathers[2 * j + h])
            convs.append(value[:, :CHUNK].reshape(shape))
            dzetas.append(value[:, CHUNK:].reshape(shape))
        outs.append((convs, dzetas))
        for i in range(2):
            rows = slice(32 * j + 16 * i, 32 * j + 16 * (i + 1))
            send_ref[:, rows, :] = jnp.concatenate(outs[j][i], axis=1).astype(BF16)
        rows = pl.ds(32 * j, 32)
        pltpu.make_async_copy(send_ref.at[:, rows], send_hbm.at[:, rows], sems.at[0]).start()
    merged = []
    for i in range(2):
        merged.append(outs[0][i][0])
        for g in range(1, 4):
            value = turn(outs[g // 2][i][g % 2], SLOT * g)
            merged[i] = jnp.where(lane < SLOT * g, merged[i], value)
    conv, dzeta = [take(x, PLACE_OUT) for x in merged]
    place = lane % SLOT
    heads = jnp.where(
        place < 2,
        conv * turn(halo, -6),
        jnp.where(place < 4, turn(dzeta, 2) * turn(feat, -2), turn(dzeta, 4) * turn(feat, 2)),
    )
    after = jnp.concatenate([heads[1:], jnp.zeros((1, 8, CHUNK), F32)], axis=0)
    terms = take(jnp.where(place < 8, feat, turn(after, 8)), ORDER_OUT)
    send_ref[:, 64:72, :] = terms.astype(BF16)
    rows = pl.ds(64, 8)
    last = pltpu.make_async_copy(send_ref.at[:, rows], send_hbm.at[:, rows], sems.at[1])
    last.start()
    rows = pl.ds(0, 64)
    pltpu.make_async_copy(send_ref.at[:, rows], send_hbm.at[:, rows], sems.at[0]).wait()
    last.wait()


def grad_filter_kernel(
    taps_hbm,
    br_hbm,
    go_hbm,
    corr_ref,
    lhs2_ref,
    inv_ref,
    twist_ref,
    out_ref,
    taps_ref,
    rows_ref,
    br_ref,
    sems,
):
    channels = go_hbm.shape[1]
    copies = [
        pltpu.make_async_copy(taps_slice(taps_hbm, channels), taps_ref, sems.at[0]),
        pltpu.make_async_copy(br_hbm.at[1:3], br_ref, sems.at[1]),
        pltpu.make_async_copy(go_hbm, rows_ref.at[2], sems.at[2]),
    ]
    for copy in copies:
        copy.start()
    for copy in copies:
        copy.wait()
    for i in range(channels // CB):
        cols = pl.ds(i * CB, CB)
        for b in range(2):
            taps = [taps_ref[b + 1, j : j + 1, cols] for j in range(3)]
            rows_ref[b, :, cols] = featurize(br_ref[b, :, cols].astype(F32), taps)[0].astype(BF16)
    scale = (BLOCKS * CHUNK) ** -0.5
    for pair in range(2):
        spectra = [
            [corr_ref[2 * pair + i, HALF * ch : HALF * (ch + 1)] for i in range(2)]
            for ch in range(GROUP)
        ]
        values = backward(spectra, lhs2_ref, twist_ref, inv_ref)
        for i in range(2):
            at = GROUP * (2 * pair + i)
            for n, m in enumerate(ORDER_OUT):
                out_ref[at : at + GROUP, CHUNK * m : CHUNK * (m + 1)] = (
                    values[i][GROUP * n : GROUP * (n + 1)] * scale
                )


def tail_block(taps_ref, rows_ref, recv_ref, out_ref, at, size):
    cols = pl.ds(at, size)
    row8 = lax.broadcasted_iota(jnp.int32, (8, size), 0)
    places = PLACE_OUT[at // 32 : (at + size) // 32]
    conv = [recv_ref[p, i : i + 16, :] for p in places for i in (0, 32)]
    dzeta = [recv_ref[p, i : i + 16, :] for p in places for i in (16, 48)]
    conv = jnp.concatenate(conv, axis=0).T.astype(F32)
    dzeta = jnp.concatenate(dzeta, axis=0).T.astype(F32)
    halo = jnp.stack([recv_ref[p, 64:72, :] for p in places]).astype(F32)
    turned = [halo] + [pltpu.roll(halo, CHUNK - SLOT * q, 2) for q in range(1, 4)]
    halo = jnp.concatenate(turned, axis=1).reshape(size, CHUNK).T
    heads, nexts = halo[:8], halo[8:16]

    def with_head(b, at):
        value = rows_ref[b, :, cols].astype(F32)
        first = jnp.where(row8 < 2, pltpu.roll(heads, 8 - at, 0), value[:8])
        return jnp.concatenate([first, value[8:]], axis=0)

    key = with_head(0, 2)
    value = with_head(1, 4)
    grads = (rows_ref[2, :, cols].astype(F32) * conv, dzeta * value, dzeta * key)
    for b in range(3):
        d = grads[b]
        s0, s1, s2 = (taps_ref[b, j : j + 1, cols] for j in range(3))
        d1 = pltpu.roll(d, CHUNK - 1, 0)
        d2 = pltpu.roll(d, CHUNK - 2, 0)
        e1 = jnp.where(row8 < 7, d1[-8:], pltpu.roll(nexts, (7 - 2 * b) % 8, 0))
        e2 = jnp.where(row8 < 6, d2[-8:], pltpu.roll(nexts, (6 - 2 * b) % 8, 0))
        d1 = jnp.concatenate([d1[:-8], e1], axis=0)
        d2 = jnp.concatenate([d2[:-8], e2], axis=0)
        out_ref[b, :, cols] = (s0 * d + s1 * d1 + s2 * d2).astype(BF16)


def tail_kernel(taps_ref, rows_ref, recv_ref, out_hbm, out_ref, sem):
    at = 0
    for part in TAIL_PARTS:
        size = out_ref.shape[2] * part // 8
        tail_block(taps_ref, rows_ref, recv_ref, out_ref, at, size)
        cols = pl.ds(at, size)
        pltpu.make_async_copy(out_ref.at[:, :, cols], out_hbm.at[:, :, cols], sem).start()
        at += size
    pltpu.make_async_copy(out_ref, out_hbm, sem).wait()


def params(mib):
    return pltpu.CompilerParams(vmem_limit_bytes=mib << 20)


def exchange(x, order):
    return lax.all_to_all(
        x, "ctx", split_axis=0, concat_axis=0, axis_index_groups=[order], tiled=True
    )


def per_device(branches, short_taps, long_filter, grad_out):
    lhs1, lhs2, fwd, inv, twist = (jnp.asarray(t) for t in tables())
    tokens, channels = grad_out.shape
    half = GROUP * HALF
    hbm = pl.BlockSpec(memory_space=pltpu.HBM)
    vmem = pl.BlockSpec(memory_space=pltpu.VMEM)
    dma = pltpu.SemaphoreType.DMA
    wire = (BLOCKS, ROWS, CHUNK)
    spectral = (32 // GROUP, half, 2 * CHUNK)
    held = lambda x: pltpu.with_memory_space_constraint(x, pltpu.HBM)
    branches, short_taps, grad_out = map(held, (branches, short_taps, grad_out))
    send = pl.pallas_call(
        head_kernel,
        in_specs=[hbm, hbm, hbm],
        out_specs=hbm,
        out_shape=pltpu.HBM(wire, BF16),
        scratch_shapes=[
            pltpu.VMEM((3, 3, channels), F32),
            pltpu.VMEM((4, tokens, channels), BF16),
            pltpu.VMEM((2, 8, channels), F32),
            pltpu.VMEM(wire, BF16),
            dma,
            dma((3,)),
            dma,
        ],
        compiler_params=params(24),
        name="head",
    )(short_taps, branches, grad_out)
    spectrum = pl.pallas_call(
        filter_kernel,
        in_specs=[vmem] * 4,
        out_specs=vmem,
        out_shape=pltpu.VMEM(spectral, BF16),
        compiler_params=params(32),
        name="filter_spectrum",
    )(long_filter, lhs1, fwd, twist)
    recv = exchange(send, ORDER_IN)
    back, corr = pl.pallas_call(
        middle_kernel,
        in_specs=[vmem] * 7,
        out_specs=[hbm, vmem],
        out_shape=[pltpu.HBM(wire, BF16), pltpu.VMEM(spectral, BF16)],
        scratch_shapes=[pltpu.VMEM(wire, BF16), dma((2,))],
        compiler_params=params(32),
        name="middle",
    )(recv, spectrum, lhs1, lhs2, fwd, inv, twist)
    grad_filter, taps, rows = pl.pallas_call(
        grad_filter_kernel,
        in_specs=[hbm, hbm, hbm, vmem, vmem, vmem, vmem],
        out_specs=[vmem, vmem, vmem],
        out_shape=[
            jax.ShapeDtypeStruct(long_filter.shape, F32),
            pltpu.VMEM((3, 3, channels), F32),
            pltpu.VMEM((3, tokens, channels), BF16),
        ],
        scratch_shapes=[
            pltpu.VMEM((2, tokens, channels), BF16),
            dma((3,)),
        ],
        compiler_params=params(32),
        name="grad_filter",
    )(short_taps, branches, grad_out, corr, lhs2, inv, twist)
    returned = exchange(back, ORDER_OUT)
    grads = pl.pallas_call(
        tail_kernel,
        in_specs=[vmem, vmem, vmem],
        out_specs=hbm,
        out_shape=pltpu.HBM(branches.shape, BF16),
        scratch_shapes=[pltpu.VMEM(branches.shape, BF16), dma],
        compiler_params=params(24),
        name="tail",
    )(taps, rows, returned)
    return grads, grad_filter


def solution(mesh):
    in_specs = (P(None, "ctx", "tp"), P(), P(("tp", "ctx"), None), P("ctx", "tp"))
    out_specs = (P(None, "ctx", "tp"), P(("tp", "ctx"), None))
    return jax.shard_map(
        per_device, mesh=mesh, in_specs=in_specs, out_specs=out_specs, check_vma=False
    )
```

```python
import functools

import jax
import jax.numpy as jnp
import ml_dtypes
import numpy as np
from jax import lax
from jax.experimental import pallas as pl
from jax.experimental.pallas import tpu as pltpu
from jax.sharding import PartitionSpec as P

F32 = jnp.float32
BF16 = jnp.bfloat16
CHUNK = 128
BLOCKS = 32
GROUP = 8
SLOT = 16
HALF = BLOCKS
PERIOD = 2 * BLOCKS * CHUNK
ROWS = 72
CB = 256
TAIL_PARTS = (3, 2, 2, 1)
KB = 128


def ctx_order(turn):
    lexical = [8 * z + 2 * (turn * y % 4) + x for y in range(4) for x in range(2) for z in range(4)]
    return [lexical[13 * j % BLOCKS] ^ 21 for j in range(BLOCKS)]


ORDER_IN = ctx_order(1)
ORDER_OUT = ctx_order(1)
PLACE_IN = [ORDER_IN.index(i) for i in range(BLOCKS)]
PLACE_OUT = [ORDER_OUT.index(i) for i in range(BLOCKS)]


@functools.lru_cache(maxsize=None)
def tables():
    bf = ml_dtypes.bfloat16
    k = np.arange(HALF)[:, None] + 0.5
    m = np.arange(BLOCKS)[None, :]
    eye = np.eye(GROUP)
    phase = 2 * np.pi * k * m / (2 * BLOCKS)
    first = np.stack([np.cos(phase), -np.sin(phase)])
    lhs1 = np.einsum("qkm,st->sqkmt", first[:, :, ORDER_IN], eye).reshape(2 * GROUP * HALF, BLOCKS * GROUP)
    last = np.stack([np.cos(phase), -np.sin(phase)]) * (2.0 / PERIOD)
    lhs2 = np.einsum("qkm,st->mstqk", last[:, :, ORDER_OUT], eye).reshape(BLOCKS * GROUP, 2 * GROUP * HALF)
    r = np.arange(CHUNK)
    cr = 2 * np.pi * (np.outer(r, r) % CHUNK) / CHUNK
    c, s = np.cos(cr), np.sin(cr)
    fwd = np.block([[c, -s], [s, c]])
    inv = np.block([[c, s], [-s, c]])
    tw = 2 * np.pi * k * r[None, :] / PERIOD
    twist = np.stack([np.cos(tw), -np.sin(tw)]).astype(np.float32)
    return lhs1.astype(bf), lhs2.astype(bf), fwd.astype(bf), inv.astype(bf), twist


def take(x, order):
    return jnp.concatenate([x[i : i + 1] for i in order], axis=0)


def runs(places):
    found = []
    for p in sorted(places):
        if found and sum(found[-1]) == p:
            found[-1] = (found[-1][0], found[-1][1] + 1)
        else:
            found.append((p, 1))
    return found


def dot(a, b):
    return jnp.dot(a, b, preferred_element_type=F32)


def taps_slice(taps_ref, channels):
    return taps_ref.at[:, :, pl.ds(pl.multiple_of(lax.axis_index("tp") * channels, 128), channels)]


def featurize(x, taps):
    s0, s1, s2 = taps
    x1 = pltpu.roll(x, 1, 0)
    x2 = pltpu.roll(x, 2, 0)
    feat = s0 * x[8:] + s1 * x1[8:] + s2 * x2[8:]
    row = lax.broadcasted_iota(jnp.int32, (8, x.shape[1]), 0)
    one, two = s1 * x1[:8], s2 * x2[:8]
    first = s0 * x[:8] + jnp.where(row < 1, 0.0, one) + jnp.where(row < 2, 0.0, two)
    tail = jnp.where(row < 1, one, 0.0) + jnp.where(row < 2, two, 0.0)
    return jnp.concatenate([first, feat], axis=0), tail


def head_feat(taps_ref, rows_ref, b, cols):
    taps = [taps_ref[b, j : j + 1, cols] for j in range(3)]
    return featurize(rows_ref[b, :, cols].astype(F32), taps)


def head_store(send_ref, at, rows, value):
    value = value.astype(BF16).T.reshape(KB // 32, 32, CHUNK)
    for n in range(KB // 32):
        send_ref[PLACE_IN[at // 32 + n], rows, :] = value[n]


def head_products(taps_ref, rows_ref, terms_ref, send_ref, at):
    cols = pl.ds(at, KB)
    key, key_tail = head_feat(taps_ref, rows_ref, 1, cols)
    value, value_tail = head_feat(taps_ref, rows_ref, 2, cols)
    head_store(send_ref, at, slice(0, 32), key * value)
    row8 = lax.broadcasted_iota(jnp.int32, (8, KB), 0)
    for i, (k, v) in enumerate(((key[:8], value[:8]), (key_tail, value_tail))):
        terms_ref[i, :, cols] = jnp.where(row8 < 4, pltpu.roll(k, 2, 0), pltpu.roll(v, 4, 0))


def head_gate_grad(taps_ref, rows_ref, terms_ref, send_ref, at):
    cols = pl.ds(at, KB)
    query, query_tail = head_feat(taps_ref, rows_ref, 0, cols)
    go = rows_ref[3, :, cols].astype(F32)
    head_store(send_ref, at, slice(32, 64), go * query)
    row8 = lax.broadcasted_iota(jnp.int32, (8, KB), 0)
    heads = jnp.where(row8 < 6, terms_ref[0, :, cols], pltpu.roll(go[:8], 6, 0))
    heads = jnp.where(row8 < 2, query[:8], heads)
    ends = jnp.where(row8 < 2, query_tail, terms_ref[1, :, cols])
    quarter = lax.broadcasted_iota(jnp.int32, (8, KB), 1) // 8 % 4
    padded = []
    for q in range(4):
        padded += [jnp.where(quarter == q, heads, 0.0), jnp.where(quarter == q, ends, 0.0)]
    padded.append(jnp.zeros((CHUNK - 64, KB), F32))
    terms = jnp.concatenate(padded, axis=0).T.reshape(KB // 32, 4, 8, CHUNK)
    terms = (terms[:, 0] + terms[:, 1] + terms[:, 2] + terms[:, 3]).astype(BF16)
    for n in range(KB // 32):
        send_ref[PLACE_IN[at // 32 + n], 64:72, :] = terms[n]


def head_kernel(
    taps_hbm,
    br_hbm,
    go_hbm,
    send_hbm,
    taps_ref,
    rows_ref,
    terms_ref,
    send_ref,
    taps_sem,
    in_sem,
    out_sem,
):
    channels = rows_ref.shape[2]
    taps_copy = pltpu.make_async_copy(taps_slice(taps_hbm, channels), taps_ref, taps_sem)
    pair_copy = pltpu.make_async_copy(br_hbm.at[1:3], rows_ref.at[1:3], in_sem.at[0])
    query_copy = pltpu.make_async_copy(br_hbm.at[0], rows_ref.at[0], in_sem.at[1])
    go_copy = pltpu.make_async_copy(go_hbm, rows_ref.at[3], in_sem.at[2])
    for copy in (taps_copy, pair_copy, query_copy, go_copy):
        copy.start()
    taps_copy.wait()
    pair_copy.wait()
    for at in range(0, channels, KB):
        head_products(taps_ref, rows_ref, terms_ref, send_ref, at)
    query_copy.wait()
    go_copy.wait()
    for at in range(0, channels, KB):
        head_gate_grad(taps_ref, rows_ref, terms_ref, send_ref, at)
        for first, length in runs(PLACE_IN[at // 32 : (at + KB) // 32]):
            out = pl.ds(first, length)
            pltpu.make_async_copy(send_ref.at[out], send_hbm.at[out], out_sem).start()
    pltpu.make_async_copy(send_ref, send_hbm, out_sem).wait()


def spread(signals, lhs1_ref, twist_ref):
    c, s = twist_ref[0], twist_ref[1]
    first = dot(lhs1_ref[...], jnp.concatenate(signals, axis=1))
    turned = []
    for ch in range(GROUP):
        at = 2 * HALF * ch
        for i in range(len(signals)):
            lanes = slice(CHUNK * i, CHUNK * (i + 1))
            re, im = first[at : at + HALF, lanes], first[at + HALF : at + 2 * HALF, lanes]
            pair = [(re * c - im * s).astype(BF16), (re * s + im * c).astype(BF16)]
            turned.append(jnp.concatenate(pair, axis=1))
    return jnp.concatenate(turned, axis=0)


def forward(signals, lhs1_ref, twist_ref, fwd_ref, apply):
    count = len(signals)
    spectra = dot(spread(signals, lhs1_ref, twist_ref), fwd_ref[...])
    for n in range(GROUP):
        apply(n, [spectra[HALF * (n * count + i) :][:HALF] for i in range(count)])


def gather(value, count, twist_ref):
    c, s = twist_ref[0], twist_ref[1]
    turned = []
    for n in range(GROUP):
        res, ims = [], []
        for i in range(count):
            part = value[HALF * (n * count + i) :][:HALF]
            re, im = part[:, :CHUNK], part[:, CHUNK:]
            res.append((re * c + im * s).astype(BF16))
            ims.append((im * c - re * s).astype(BF16))
        turned.append(jnp.concatenate(res, axis=1))
        turned.append(jnp.concatenate(ims, axis=1))
    return jnp.concatenate(turned, axis=0)


def backward(spectra, lhs2_ref, twist_ref, inv_ref):
    count = len(spectra[0])
    value = dot(jnp.concatenate([x for ch in spectra for x in ch], axis=0), inv_ref[...])
    both = dot(lhs2_ref[...], gather(value, count, twist_ref))
    return [both[:, CHUNK * i : CHUNK * (i + 1)] for i in range(count)]


def filter_kernel(filter_ref, lhs1_ref, fwd_ref, twist_ref, out_ref):
    scale = (BLOCKS * CHUNK) ** -0.5
    for pair in range(2):
        signals = []
        for g in (2 * pair, 2 * pair + 1):
            rows = filter_ref[GROUP * g : GROUP * (g + 1), :] * scale
            stacked = [rows[:, CHUNK * m : CHUNK * (m + 1)] for m in ORDER_IN]
            signals.append(jnp.concatenate(stacked, axis=0).astype(BF16))

        def store(ch, parts):
            rows = slice(HALF * ch, HALF * (ch + 1))
            for i in range(2):
                out_ref[2 * pair + i, rows] = parts[i].astype(BF16)

        forward(signals, lhs1_ref, twist_ref, fwd_ref, store)


def middle_kernel(
    recv_ref,
    spec_ref,
    lhs1_ref,
    lhs2_ref,
    fwd_ref,
    inv_ref,
    twist_ref,
    send_hbm,
    corr_ref,
    send_ref,
    sems,
):
    shape = (BLOCKS, GROUP, CHUNK)
    flat = (BLOCKS * GROUP, CHUNK)
    lane = lax.broadcasted_iota(jnp.int32, (GROUP, CHUNK), 1)
    turn = lambda x, by: pltpu.roll(x, by % CHUNK, 2)
    halo = take(recv_ref[:, 64:72, :].astype(F32), PLACE_IN)
    before = jnp.concatenate([jnp.zeros((1, 8, CHUNK), F32), halo[:-1]], axis=0)
    feat = halo + turn(before, -8)
    prod = take(turn(feat, -2) * turn(feat, -4), ORDER_IN)
    gate = take(feat * turn(halo, -6), ORDER_IN)
    outs, mixes, spreads = [], [], []
    join = lambda re, im: jnp.concatenate([re.astype(BF16), im.astype(BF16)], axis=1)
    for j in range(2):
        both = [recv_ref[:, at + 16 * j : at + 16 * (j + 1), :].astype(F32) for at in (0, 32)]
        for h in range(2):
            g = 2 * j + h
            rows = slice(GROUP * h, GROUP * (h + 1))
            signals = []
            for x, fix in zip(both, (prod, gate)):
                fixed = jnp.where(lane < 2, turn(fix, -SLOT * g), x[:, rows])
                signals.append(fixed.reshape(flat).astype(BF16))
            spreads.append(spread(signals, lhs1_ref, twist_ref))
    size = 2 * GROUP * HALF
    everything = dot(jnp.concatenate(spreads, axis=0), fwd_ref[...])
    for g in range(4):
        spectra = everything[size * g : size * (g + 1)]
        mixed = []
        for ch in range(GROUP):
            at = 2 * HALF * ch
            parts = (spectra[at : at + HALF], spectra[at + HALF : at + 2 * HALF])
            (pr, pi), (gr, gi) = [(x[:, :CHUNK], x[:, CHUNK:]) for x in parts]
            rows = slice(HALF * ch, HALF * (ch + 1))
            hr = spec_ref[g, rows, :CHUNK].astype(F32)
            hi = spec_ref[g, rows, CHUNK:].astype(F32)
            corr_ref[g, rows] = join(pr * gr + pi * gi, pr * gi - pi * gr)
            mixed.append(join(hr * pr - hi * pi, hr * pi + hi * pr))
            mixed.append(join(hr * gr + hi * gi, hr * gi - hi * gr))
        mixes.append(jnp.concatenate(mixed, axis=0))
    everything = dot(jnp.concatenate(mixes, axis=0), inv_ref[...])
    gathers = [gather(everything[size * g : size * (g + 1)], 2, twist_ref) for g in range(4)]
    for j in range(2):
        convs, dzetas = [], []
        for h in range(2):
            value = dot(lhs2_ref[...], gathers[2 * j + h])
            convs.append(value[:, :CHUNK].reshape(shape))
            dzetas.append(value[:, CHUNK:].reshape(shape))
        outs.append((convs, dzetas))
        for i in range(2):
            rows = slice(32 * j + 16 * i, 32 * j + 16 * (i + 1))
            send_ref[:, rows, :] = jnp.concatenate(outs[j][i], axis=1).astype(BF16)
        rows = pl.ds(32 * j, 32)
        pltpu.make_async_copy(send_ref.at[:, rows], send_hbm.at[:, rows], sems.at[0]).start()
    merged = []
    for i in range(2):
        merged.append(outs[0][i][0])
        for g in range(1, 4):
            value = turn(outs[g // 2][i][g % 2], SLOT * g)
            merged[i] = jnp.where(lane < SLOT * g, merged[i], value)
    conv, dzeta = [take(x, PLACE_OUT) for x in merged]
    place = lane % SLOT
    heads = jnp.where(
        place < 2,
        conv * turn(halo, -6),
        jnp.where(place < 4, turn(dzeta, 2) * turn(feat, -2), turn(dzeta, 4) * turn(feat, 2)),
    )
    after = jnp.concatenate([heads[1:], jnp.zeros((1, 8, CHUNK), F32)], axis=0)
    terms = take(jnp.where(place < 8, feat, turn(after, 8)), ORDER_OUT)
    send_ref[:, 64:72, :] = terms.astype(BF16)
    rows = pl.ds(64, 8)
    last = pltpu.make_async_copy(send_ref.at[:, rows], send_hbm.at[:, rows], sems.at[1])
    last.start()
    rows = pl.ds(0, 64)
    pltpu.make_async_copy(send_ref.at[:, rows], send_hbm.at[:, rows], sems.at[0]).wait()
    last.wait()


def grad_filter_kernel(
    taps_hbm,
    br_hbm,
    go_hbm,
    corr_ref,
    lhs2_ref,
    inv_ref,
    twist_ref,
    out_ref,
    taps_ref,
    rows_ref,
    br_ref,
    sems,
):
    channels = go_hbm.shape[1]
    copies = [
        pltpu.make_async_copy(taps_slice(taps_hbm, channels), taps_ref, sems.at[0]),
        pltpu.make_async_copy(br_hbm.at[1:3], br_ref, sems.at[1]),
        pltpu.make_async_copy(go_hbm, rows_ref.at[2], sems.at[2]),
    ]
    for copy in copies:
        copy.start()
    for copy in copies:
        copy.wait()
    for i in range(channels // CB):
        cols = pl.ds(i * CB, CB)
        for b in range(2):
            taps = [taps_ref[b + 1, j : j + 1, cols] for j in range(3)]
            rows_ref[b, :, cols] = featurize(br_ref[b, :, cols].astype(F32), taps)[0].astype(BF16)
    scale = (BLOCKS * CHUNK) ** -0.5
    for pair in range(2):
        spectra = [
            [corr_ref[2 * pair + i, HALF * ch : HALF * (ch + 1)] for i in range(2)]
            for ch in range(GROUP)
        ]
        values = backward(spectra, lhs2_ref, twist_ref, inv_ref)
        for i in range(2):
            at = GROUP * (2 * pair + i)
            for n, m in enumerate(ORDER_OUT):
                out_ref[at : at + GROUP, CHUNK * m : CHUNK * (m + 1)] = (
                    values[i][GROUP * n : GROUP * (n + 1)] * scale
                )


def tail_block(taps_ref, rows_ref, recv_ref, out_ref, at, size):
    cols = pl.ds(at, size)
    row8 = lax.broadcasted_iota(jnp.int32, (8, size), 0)
    places = PLACE_OUT[at // 32 : (at + size) // 32]
    conv = [recv_ref[p, i : i + 16, :] for p in places for i in (0, 32)]
    dzeta = [recv_ref[p, i : i + 16, :] for p in places for i in (16, 48)]
    conv = jnp.concatenate(conv, axis=0).T.astype(F32)
    dzeta = jnp.concatenate(dzeta, axis=0).T.astype(F32)
    halo = jnp.stack([recv_ref[p, 64:72, :] for p in places]).astype(F32)
    turned = [halo] + [pltpu.roll(halo, CHUNK - SLOT * q, 2) for q in range(1, 4)]
    halo = jnp.concatenate(turned, axis=1).reshape(size, CHUNK).T
    heads, nexts = halo[:8], halo[8:16]

    def with_head(b, at):
        value = rows_ref[b, :, cols].astype(F32)
        first = jnp.where(row8 < 2, pltpu.roll(heads, 8 - at, 0), value[:8])
        return jnp.concatenate([first, value[8:]], axis=0)

    key = with_head(0, 2)
    value = with_head(1, 4)
    grads = (rows_ref[2, :, cols].astype(F32) * conv, dzeta * value, dzeta * key)
    for b in range(3):
        d = grads[b]
        s0, s1, s2 = (taps_ref[b, j : j + 1, cols] for j in range(3))
        d1 = pltpu.roll(d, CHUNK - 1, 0)
        d2 = pltpu.roll(d, CHUNK - 2, 0)
        e1 = jnp.where(row8 < 7, d1[-8:], pltpu.roll(nexts, (7 - 2 * b) % 8, 0))
        e2 = jnp.where(row8 < 6, d2[-8:], pltpu.roll(nexts, (6 - 2 * b) % 8, 0))
        d1 = jnp.concatenate([d1[:-8], e1], axis=0)
        d2 = jnp.concatenate([d2[:-8], e2], axis=0)
        out_ref[b, :, cols] = (s0 * d + s1 * d1 + s2 * d2).astype(BF16)


def tail_kernel(taps_ref, rows_ref, recv_ref, out_hbm, out_ref, sem):
    at = 0
    for part in TAIL_PARTS:
        size = out_ref.shape[2] * part // 8
        tail_block(taps_ref, rows_ref, recv_ref, out_ref, at, size)
        cols = pl.ds(at, size)
        pltpu.make_async_copy(out_ref.at[:, :, cols], out_hbm.at[:, :, cols], sem).start()
        at += size
    pltpu.make_async_copy(out_ref, out_hbm, sem).wait()


def params(mib):
    return pltpu.CompilerParams(vmem_limit_bytes=mib << 20)


def exchange(x, order):
    return lax.all_to_all(
        x, "ctx", split_axis=0, concat_axis=0, axis_index_groups=[order], tiled=True
    )


def per_device(branches, short_taps, long_filter, grad_out):
    lhs1, lhs2, fwd, inv, twist = (jnp.asarray(t) for t in tables())
    tokens, channels = grad_out.shape
    half = GROUP * HALF
    hbm = pl.BlockSpec(memory_space=pltpu.HBM)
    vmem = pl.BlockSpec(memory_space=pltpu.VMEM)
    dma = pltpu.SemaphoreType.DMA
    wire = (BLOCKS, ROWS, CHUNK)
    spectral = (32 // GROUP, half, 2 * CHUNK)
    held = lambda x: pltpu.with_memory_space_constraint(x, pltpu.HBM)
    branches, short_taps, grad_out = map(held, (branches, short_taps, grad_out))
    send = pl.pallas_call(
        head_kernel,
        in_specs=[hbm, hbm, hbm],
        out_specs=hbm,
        out_shape=pltpu.HBM(wire, BF16),
        scratch_shapes=[
            pltpu.VMEM((3, 3, channels), F32),
            pltpu.VMEM((4, tokens, channels), BF16),
            pltpu.VMEM((2, 8, channels), F32),
            pltpu.VMEM(wire, BF16),
            dma,
            dma((3,)),
            dma,
        ],
        compiler_params=params(24),
        name="head",
    )(short_taps, branches, grad_out)
    spectrum = pl.pallas_call(
        filter_kernel,
        in_specs=[vmem] * 4,
        out_specs=vmem,
        out_shape=pltpu.VMEM(spectral, BF16),
        compiler_params=params(32),
        name="filter_spectrum",
    )(long_filter, lhs1, fwd, twist)
    recv = exchange(send, ORDER_IN)
    back, corr = pl.pallas_call(
        middle_kernel,
        in_specs=[vmem] * 7,
        out_specs=[hbm, vmem],
        out_shape=[pltpu.HBM(wire, BF16), pltpu.VMEM(spectral, BF16)],
        scratch_shapes=[pltpu.VMEM(wire, BF16), dma((2,))],
        compiler_params=params(32),
        name="middle",
    )(recv, spectrum, lhs1, lhs2, fwd, inv, twist)
    grad_filter, taps, rows = pl.pallas_call(
        grad_filter_kernel,
        in_specs=[hbm, hbm, hbm, vmem, vmem, vmem, vmem],
        out_specs=[vmem, vmem, vmem],
        out_shape=[
            jax.ShapeDtypeStruct(long_filter.shape, F32),
            pltpu.VMEM((3, 3, channels), F32),
            pltpu.VMEM((3, tokens, channels), BF16),
        ],
        scratch_shapes=[
            pltpu.VMEM((2, tokens, channels), BF16),
            dma((3,)),
        ],
        compiler_params=params(32),
        name="grad_filter",
    )(short_taps, branches, grad_out, corr, lhs2, inv, twist)
    returned = exchange(back, ORDER_OUT)
    grads = pl.pallas_call(
        tail_kernel,
        in_specs=[vmem, vmem, vmem],
        out_specs=hbm,
        out_shape=pltpu.HBM(branches.shape, BF16),
        scratch_shapes=[pltpu.VMEM(branches.shape, BF16), dma],
        compiler_params=params(24),
        name="tail",
    )(taps, rows, returned)
    return grads, grad_filter


def solution(mesh):
    in_specs = (P(None, "ctx", "tp"), P(), P(("tp", "ctx"), None), P("ctx", "tp"))
    out_specs = (P(None, "ctx", "tp"), P(("tp", "ctx"), None))
    return jax.shard_map(
        per_device, mesh=mesh, in_specs=in_specs, out_specs=out_specs, check_vma=False
    )
```
